128 devices in a mesh: dp: 4 (over y), mp: 32 (over x, z, core).
Axes of the slice: x: 4, y: 4, z: 4, core: 2. Of those that a mesh axis runs over, the one named last changes fastest.
Arguments:
- residual_in: bfloat16 [512, 3584], P('dp', 'mp'), may hold values from -6 to 6
- pre_gain: float32 [3584], replicated, may hold values from 0.5 to 1.5
- post_gain: float32 [3584], replicated, may hold values from 0.5 to 1.5
- w_gate: bfloat16 [3584, 14336], P(None, 'mp'), may hold values from -0.09375 to 0.09375
- w_up: bfloat16 [3584, 14336], P(None, 'mp'), may hold values from -0.09375 to 0.09375
- w_down: bfloat16 [14336, 3584], P('mp'), may hold values from -0.046875 to 0.046875
- w_enc: bfloat16 [3584, 65536], P(None, ('dp', 'mp')), may hold values from -0.09375 to 0.09375
- b_enc: float32 [65536], P(('dp', 'mp')), may hold values from -2.5 to 2.5
- threshold: float32 [65536], P(('dp', 'mp')), may hold values from 0.1 to 1
- w_dec: bfloat16 [65536, 3584], P(('dp', 'mp')), may hold values from -0.0234375 to 0.0234375
- b_dec: float32 [3584], replicated, may hold values from -1.5 to 1.5
Outputs:
- loss_value: float32 [], replicated
- d_w_enc: bfloat16 [3584, 65536], P(None, ('dp', 'mp'))
- d_w_dec: bfloat16 [65536, 3584], P(('dp', 'mp'))
- d_b_enc: float32 [65536], P(('dp', 'mp'))
- d_threshold: float32 [65536], P(('dp', 'mp'))
- d_b_dec: float32 [3584], replicated
The draws below stay inside these ranges and needn't reach their ends.
All inputs are finite; a program needn't handle non-finite values.
Results may differ from the reference program's by a relative error of at most 0.014.
The reference program's roundings to bfloat16 on the way count: a program that leaves them out, or rounds other values in their place, can miss the bound.
Values may be sent and summed in bfloat16 or wider, within the bound.
A program may use at most 128 MiB of HBM per device.

```python
import math
import jax
import jax.numpy as jnp
from jax import lax

D = 3584
FF = 14336
TOKENS = 512
FEATURES = 65536


def draw_b_enc(key, part):
    position = (jnp.arange(FEATURES).astype(jnp.float32) + 0.5) / FEATURES
    noise = 0.3 * jax.random.normal(jax.random.fold_in(key, 11), (FEATURES,), jnp.float32)
    values = -2.0 + 4.0 * position + noise
    return jnp.clip(values, -2.5, 2.5).astype(jnp.float32)


def steps_of(own_key, extent, pieces, low, top_value):
    def one(axis_at, blocks):
        draws = jax.random.uniform(jax.random.fold_in(jax.random.fold_in(own_key, 6), axis_at), (blocks,), jnp.float32, low / len(pieces), top_value / len(pieces))
        return jnp.repeat(jnp.exp(draws), extent[axis_at] // blocks).reshape((-1,) + (1,) * (len(extent) - axis_at - 1))

    level = one(*pieces[0])
    for cut in pieces[1:]:
        level = level * one(*cut)
    return level


def gaussian(own_key, dims, deviation, most, pieces=(), held_as=jnp.bfloat16):
    level = steps_of(own_key, dims, pieces, -0.22, 0.18) if pieces else 1.0
    entries = jax.random.normal(own_key, dims, jnp.float32) * deviation * level
    return jnp.minimum(jnp.maximum(entries, -most), most).astype(held_as)


def setup_inputs(seed: int = 0) -> dict:
    splits = jax.random.split(jax.random.key(seed), 12)
    residual_in = gaussian(splits[0], (TOKENS, D), 1.0, 6.0, ((0, 4), (1, 32)))
    pre_gain = jnp.clip(1.0 + 0.1 * jax.random.normal(splits[1], (D,), jnp.float32), 0.5, 1.5)
    post_gain = jnp.clip(1.0 + 0.1 * jax.random.normal(splits[2], (D,), jnp.float32), 0.5, 1.5)
    w_gate = gaussian(splits[3], (D, FF), D ** -0.5, 0.09375, ((1, 32),))
    w_up = gaussian(splits[4], (D, FF), D ** -0.5, 0.09375, ((1, 32),))
    w_down = gaussian(splits[5], (FF, D), FF ** -0.5, 0.046875, ((0, 32),))
    w_enc = gaussian(splits[6], (D, FEATURES), D ** -0.5, 0.09375, ((1, 128),))
    b_enc = draw_b_enc(jax.random.fold_in(splits[11], 71), 0)
    threshold = jnp.clip(jnp.exp(math.log(1.0) - 2.3025851 * jax.random.uniform(splits[8], (FEATURES,), jnp.float32) ** steps_of(splits[8], (FEATURES,), ((0, 128),), -0.2, 0.2)), 0.1, 1.0)
    w_dec = gaussian(splits[9], (FEATURES, D), FEATURES ** -0.5, 0.0234375, ((0, 128),))
    b_dec = gaussian(splits[10], (D,), 0.3, 1.5, (), jnp.float32)
    return dict(residual_in=residual_in, pre_gain=pre_gain, post_gain=post_gain, w_gate=w_gate, w_up=w_up, w_down=w_down, w_enc=w_enc, b_enc=b_enc, threshold=threshold, w_dec=w_dec, b_dec=b_dec)


norm_eps = 1e-06
gate_band = 0.1
sparsity_coef = 0.05

def rms_norm(values, gain):
    return values * lax.rsqrt(lax.optimization_barrier(jnp.mean(values * values, axis=-1, keepdims=True)) + norm_eps) * gain

def reference(residual_in, pre_gain, post_gain, w_gate, w_up, w_down, w_enc, b_enc, threshold, w_dec, b_dec):
    resid_wide = residual_in.astype(jnp.float32)
    normed = rms_norm(resid_wide, pre_gain).astype(jnp.bfloat16)
    gate_out = jnp.dot(normed, w_gate, preferred_element_type=jnp.float32)
    up_out = jnp.dot(normed, w_up, preferred_element_type=jnp.float32)
    hidden = (jax.nn.gelu(gate_out, approximate=True) * up_out).astype(jnp.bfloat16)
    block_out = jnp.dot(hidden, w_down, preferred_element_type=jnp.float32)
    layer_out = (resid_wide + rms_norm(block_out, post_gain)).astype(jnp.bfloat16)
    pre_act = jnp.dot(layer_out, w_enc, preferred_element_type=jnp.float32) + b_enc
    soft = jax.nn.sigmoid((pre_act - threshold) / gate_band)
    feat_bf = (pre_act * soft).astype(jnp.bfloat16)
    error_t = jnp.dot(feat_bf, w_dec, preferred_element_type=jnp.float32) + b_dec - layer_out.astype(jnp.float32)
    loss_value = (0.5 * jnp.sum(error_t * error_t) + sparsity_coef * jnp.sum(soft)) / (TOKENS * D)
    d_b_dec = lax.optimization_barrier(jnp.sum(error_t, axis=0))
    err_bf = error_t.astype(jnp.bfloat16)
    d_w_dec = jnp.dot(feat_bf.T, err_bf, preferred_element_type=jnp.float32).astype(jnp.bfloat16)
    grad_feat = jnp.dot(err_bf, w_dec.T, preferred_element_type=jnp.float32)
    slope = soft * (1.0 - soft) / gate_band
    side_term = (grad_feat * pre_act + sparsity_coef) * slope
    grad_pre = grad_feat * soft + side_term
    d_threshold = -lax.optimization_barrier(jnp.sum(side_term, axis=0))
    d_b_enc = lax.optimization_barrier(jnp.sum(grad_pre, axis=0))
    d_w_enc = jnp.dot(layer_out.T, grad_pre.astype(jnp.bfloat16), preferred_element_type=jnp.float32).astype(jnp.bfloat16)
    return (loss_value, d_w_enc, d_w_dec, d_b_enc, d_threshold, d_b_dec)
```

```python
import jax
import jax.numpy as jnp
from jax import lax
from jax.experimental import pallas as pl
from jax.experimental.pallas import tpu as pltpu
from jax.sharding import PartitionSpec as P

norm_eps = 1e-06
gate_band = 0.1
sparsity_coef = 0.05

MESH = pl.DeviceIdType.MESH
F32 = jnp.float32
BF16 = jnp.bfloat16

D = 3584
QUARTER = 896
WIDTHS = (256, 256, 384)
OFFSETS = (0, 256, 512)
ORDERS = ("xyz", "yzx", "zxy")
PIECES = (0, 1, 2)


def coordinates():
    y = lax.axis_index("dp")
    m = lax.axis_index("mp")
    return {"x": m // 8, "y": y, "z": (m // 2) % 4, "c": m % 2}


def device(at):
    return (at["y"], (at["x"] * 4 + at["z"]) * 2 + at["c"])


def moved(at, axis, steps):
    there = dict(at)
    there[axis] = (at[axis] + steps) % (2 if axis == "c" else 4)
    return there


def grid_index(at, gathered):
    return tuple(slice(None) if a in gathered else at[a] for a in "yxz")


def mlp_and_sae(
    resid, pre_gain, post_gain, b_dec, b_enc, threshold,
    wg_hbm, wu_hbm, wd_hbm, we_hbm, wdec_hbm,
    err_out0, err_out1, err_out2, l_out0, l_out1, l_out2, feat_out, pre_out, gate_out,
    wg, wu, wd, we, wdec, gath, norm_t, hidden, bp, bp_in, bs, b_in, sq, sq_in,
    l0, l1, l2, feat, pre, p0, p1, p2, pin0, pin1, pin2, s0, s1, s2,
    ra0, ra1, ra2, sa0, sa1, sa2, rb0, rb1, rb2, sb0, sb1, sb2, rc0, rc1, rc2,
    e0, e1, e2, gsum, gin,
    wsem, asend, arecv, bcsend, bcrecv, bsend, brecv, sqsend, sqrecv,
    dsend, drecv, dcsend, dcrecv, pcsend, pcrecv, rsend, rrecv,
    esend, erecv, ecsend, ecrecv, gsend, grecv, osem,
):
    at = coordinates()
    x, y, z, c = at["x"], at["y"], at["z"], at["c"]
    sibling = device(moved(at, "c", 1))
    layer = (l0, l1, l2)
    part = (p0, p1, p2)
    part_in = (pin0, pin1, pin2)
    total = (s0, s1, s2)
    in_a, sum_a = (ra0, ra1, ra2), (sa0, sa1, sa2)
    in_b, sum_b = (rb0, rb1, rb2), (sb0, sb1, sb2)
    in_c = (rc0, rc1, rc2)
    err = (e0, e1, e2)

    loads = [
        pltpu.make_async_copy(src, dst, wsem.at[i])
        for i, (src, dst) in enumerate(
            ((wg_hbm, wg), (wu_hbm, wu), (wd_hbm, wd), (we_hbm, we), (wdec_hbm, wdec))
        )
    ]
    for load in loads:
        load.start()

    plane = [(i, j) for i in range(4) for j in range(4) if i or j]
    barrier = pltpu.get_barrier_semaphore()
    greeted = [moved(moved(at, "x", i), "z", j) for i, j in plane]
    greeted += [moved(at, "y", k) for k in (1, 2, 3)] + [moved(at, "c", 1)]
    for there in greeted:
        pl.semaphore_signal(barrier, inc=1, device_id=device(there), device_id_type=MESH)
    pl.semaphore_wait(barrier, len(greeted))

    def remote(src, dst, send, recv, there):
        copy = pltpu.make_async_remote_copy(
            src_ref=src, dst_ref=dst, send_sem=send, recv_sem=recv,
            device_id=there, device_id_type=MESH,
        )
        copy.start()
        return copy

    unsent = []

    copies = []
    for n, (i, j) in enumerate(plane):
        there = moved(moved(at, "x", i), "z", j)
        copies.append(remote(resid, gath.at[x, z, c], asend.at[n], arecv.at[n], device(there)))
    gath[x, z, c] = resid[...]
    for copy in copies:
        copy.wait_recv()
    unsent += copies
    copy = remote(gath.at[:, :, c], gath.at[:, :, c], asend.at[15], arecv.at[15], sibling)
    copy.wait_recv()
    unsent.append(copy)

    squares = jnp.zeros((1, 128), F32)
    for i in range(4):
        for j in range(4):
            rows = gath[i, j].astype(F32).reshape(224, 128)
            squares = squares + jnp.sum(rows * rows, axis=0, keepdims=True)
    scale = lax.rsqrt(squares / D + norm_eps)
    gains = jnp.concatenate([pre_gain[...], jnp.zeros((100, 128), F32)], axis=0).T
    everything = gath[...].reshape(D, 128)
    for k in range(28):
        rows = everything[k * 128:(k + 1) * 128].astype(F32)
        norm_t[k * 128:(k + 1) * 128, :] = (rows * scale * gains[:, k:k + 1]).astype(BF16)

    loads[0].wait()
    loads[1].wait()
    gate = jnp.dot(wg[...], norm_t[...], preferred_element_type=F32)
    up = jnp.dot(wu[...], norm_t[...], preferred_element_type=F32)
    hidden[...] = (jax.nn.gelu(gate, approximate=True) * up).T.astype(BF16)

    loads[2].wait()
    copies = []
    for q in range(4):
        own = jnp.dot(hidden[...], wd[:, q * QUARTER:(q + 1) * QUARTER], preferred_element_type=F32)
        bp[:, :, q] = own.astype(BF16).reshape(2, 4, 16, QUARTER)
        copies.append(remote(bp.at[1 - c, :, q], bp_in.at[:, q], bcsend.at[q], bcrecv.at[q], sibling))
    for q, copy in enumerate(copies):
        copy.wait_recv()
        bs[:, q] = (bp[c, :, q].astype(F32) + bp_in[:, q].astype(F32)).astype(BF16)
    unsent += copies
    copies = []
    for n, (i, j) in enumerate(plane):
        there = moved(moved(at, "x", i), "z", j)
        copies.append(
            remote(bs.at[there["x"], there["z"]], b_in.at[n], bsend.at[n], brecv.at[n], device(there))
        )
    pick = lax.broadcasted_iota(jnp.int32, (16, 128), 0) + (c * 64 + x * 16)
    pick = (lax.broadcasted_iota(jnp.int32, (16, 128), 1) == pick).astype(BF16)
    mine = lax.dot_general(
        pick, own_rows(gath, z), (((1,), (1,)), ((), ())), preferred_element_type=F32
    )
    block = bs[x, z].astype(F32)
    for n, copy in enumerate(copies):
        copy.wait_recv()
        block = block + b_in[n].astype(F32)
    unsent += copies
    sums = jnp.broadcast_to(jnp.sum(block * block, axis=1, keepdims=True), (16, 128))
    sq[...] = sums
    copies = [
        remote(sq, sq_in.at[k - 1], sqsend.at[k - 1], sqrecv.at[k - 1], device(moved(at, "z", k)))
        for k in (1, 2, 3)
    ]
    for k, copy in enumerate(copies):
        copy.wait_recv()
        sums = sums + sq_in[k]
    unsent += copies
    row_scale = lax.rsqrt(sums[:, :1] / D + norm_eps)
    gain = lane_row(post_gain, z)
    block = mine + block * row_scale * gain
    for p in PIECES:
        layer[p][c, y, x, z] = block[:, OFFSETS[p]:OFFSETS[p] + WIDTHS[p]].astype(BF16)

    def gather(arrays, send, recv, csend, crecv):
        held = []
        stage = {}
        for step in range(3):
            for p in PIECES:
                order = ORDERS[p]
                if step:
                    for copy in stage[p]:
                        copy.wait_recv()
                here = arrays[p].at[(c,) + grid_index(at, order[:step])]
                stage[p] = [
                    remote(here, here, send.at[step, p, k - 1], recv.at[step, p, k - 1],
                           device(moved(at, order[step], k)))
                    for k in (1, 2, 3)
                ]
                held.extend(stage[p])
                if step == 2:
                    held.append(remote(here, here, csend.at[p, 0], crecv.at[p, 0], sibling))
        across = [copy for copy in held[-12:][3::4]]
        for k in (1, 2, 3):
            for p in PIECES:
                order = ORDERS[p]
                stage[p][k - 1].wait_recv()
                source = moved(at, order[2], -k)
                there = arrays[p].at[(c,) + grid_index(source, order[:2])]
                copy = remote(there, there, csend.at[p, k], crecv.at[p, k], sibling)
                held.append(copy)
                across.append(copy)
        for copy in across:
            copy.wait_recv()
        return held

    unsent += gather(layer, dsend, drecv, dcsend, dcrecv)
    outs = [
        pltpu.make_async_copy(layer[p], (l_out0, l_out1, l_out2)[p], osem.at[p]) for p in PIECES
    ]
    for out in outs:
        out.start()

    loads[3].wait()
    pre[...] = jnp.broadcast_to(b_enc[...], (512, 512))
    for q in range(4):
        for p in PIECES:
            low = q * QUARTER + OFFSETS[p]
            rows = layer[p][:, :, :, q].reshape(512, WIDTHS[p])
            pre[...] += jnp.dot(rows, we[low:low + WIDTHS[p], :], preferred_element_type=F32)
    pre_act = pre[...]
    soft = jax.nn.sigmoid((pre_act - threshold[...]) / gate_band)
    feat[...] = (pre_act * soft).astype(BF16)
    gate_sum = jnp.broadcast_to(jnp.sum(soft).reshape(1, 1), (8, 128))
    outs.append(pltpu.make_async_copy(feat, feat_out, osem.at[3]))
    outs.append(pltpu.make_async_copy(pre, pre_out, osem.at[4]))
    outs[3].start()
    outs[4].start()

    loads[4].wait()

    def partial(half):
        rows = feat[pl.ds(pl.multiple_of(half * 256, 256), 256), :]
        for q in range(4):
            for p in PIECES:
                low = q * QUARTER + OFFSETS[p]
                value = jnp.dot(rows, wdec[:, low:low + WIDTHS[p]], preferred_element_type=F32)
                part[p][half, :, :, q] = value.astype(BF16).reshape(4, 4, 16, WIDTHS[p])

    partial(1 - c)
    copies = [
        remote(part[p].at[1 - c], part_in[p], pcsend.at[p], pcrecv.at[p], sibling) for p in PIECES
    ]
    unsent += copies
    gsum[0] = gate_sum
    gate_copies = [remote(gsum.at[0], gin.at[9], gsend.at[9], grecv.at[9], sibling)]
    partial(c)
    stage = {}
    for p in PIECES:
        copies[p].wait_recv()
        for i in range(4):
            total[p][i] = (part[p][c, i].astype(F32) + part_in[p][i].astype(F32)).astype(BF16)
        axis = ORDERS[p][2]
        stage[p] = []
        for k in (1, 2, 3):
            there = moved(at, axis, k)
            src = total[p].at[grid_index(there, [a for a in "xyz" if a != axis])]
            stage[p].append(
                remote(src, in_a[p].at[k - 1], rsend.at[0, p, k - 1], rrecv.at[0, p, k - 1], device(there))
            )
        unsent += stage[p]
    gate_copies[0].wait_recv()
    gate_sum = gate_sum + gin[9]
    unsent += gate_copies

    def gate_step(s, axis, value):
        gsum[1 + s] = value
        made = [
            remote(gsum.at[1 + s], gin.at[3 * s + k - 1], gsend.at[3 * s + k - 1],
                   grecv.at[3 * s + k - 1], device(moved(at, axis, k)))
            for k in (1, 2, 3)
        ]
        return made

    def gate_finish(s, made, value):
        for k, copy in enumerate(made):
            copy.wait_recv()
            value = value + gin[3 * s + k]
        return value

    gate_copies = gate_step(0, "x", gate_sum)
    unsent += gate_copies
    for p in PIECES:
        last, second = ORDERS[p][2], ORDERS[p][1]
        for copy in stage[p]:
            copy.wait_recv()
        value = total[p][grid_index(at, [a for a in "xyz" if a != last])].astype(F32)
        for k in range(3):
            value = value + in_a[p][k].astype(F32)
        sum_a[p][...] = value.astype(BF16)
        stage[p] = []
        left = [a for a in "yxz" if a != last]
        for k in (1, 2, 3):
            there = moved(at, second, k)
            src = sum_a[p].at[tuple(there[a] if a == second else slice(None) for a in left)]
            stage[p].append(
                remote(src, in_b[p].at[k - 1], rsend.at[1, p, k - 1], rrecv.at[1, p, k - 1], device(there))
            )
        unsent += stage[p]
    gate_sum = gate_finish(0, gate_copies, gate_sum)
    gate_copies = gate_step(1, "y", gate_sum)
    unsent += gate_copies
    for p in PIECES:
        last, second, first = ORDERS[p][2], ORDERS[p][1], ORDERS[p][0]
        for copy in stage[p]:
            copy.wait_recv()
        left = [a for a in "yxz" if a != last]
        value = sum_a[p][tuple(at[a] if a == second else slice(None) for a in left)].astype(F32)
        for k in range(3):
            value = value + in_b[p][k].astype(F32)
        sum_b[p][...] = value.astype(BF16)
        stage[p] = []
        for k in (1, 2, 3):
            there = moved(at, first, k)
            stage[p].append(
                remote(sum_b[p].at[there[first]], in_c[p].at[k - 1], rsend.at[2, p, k - 1],
                       rrecv.at[2, p, k - 1], device(there))
            )
        unsent += stage[p]
    gate_sum = gate_finish(1, gate_copies, gate_sum)
    gate_copies = gate_step(2, "z", gate_sum)
    unsent += gate_copies
    bias = lane_row(b_dec, z)
    for p in PIECES:
        for copy in stage[p]:
            copy.wait_recv()
        value = sum_b[p][at[ORDERS[p][0]]].astype(F32)
        for k in range(3):
            value = value + in_c[p][k].astype(F32)
        value = value + bias[:, OFFSETS[p]:OFFSETS[p] + WIDTHS[p]]
        value = value - layer[p][c, y, x, z].astype(F32)
        err[p][c, y, x, z] = value.astype(BF16)

    unsent += gather(err, esend, erecv, ecsend, ecrecv)
    gate_sum = gate_finish(2, gate_copies, gate_sum)
    gate_out[...] = gate_sum
    for p in PIECES:
        out = pltpu.make_async_copy(err[p], (err_out0, err_out1, err_out2)[p], osem.at[5 + p])
        out.start()
        outs.append(out)
    for copy in unsent:
        copy.wait_send()
    for out in outs:
        out.wait()


def own_rows(gath, z):
    return gath[pl.ds(z, 1)].reshape(QUARTER, 128)


def lane_row(ref, z):
    rows = [ref[pl.ds(z * 7 + i, 1), :] for i in range(7)]
    return jnp.concatenate(rows, axis=1)


def gradients(
    threshold, gate_in,
    e0_hbm, e1_hbm, e2_hbm, l0_hbm, l1_hbm, l2_hbm, feat_hbm, pre_hbm, wdec_hbm,
    wenc_grad, wdec_grad, benc_grad, thresh_grad, bdec_grad, loss,
    e0, e1, e2, l0, l1, l2, feat, feat_t, pre, wdec, gfeat, gpre, odec, oenc,
    isem, dsem, esem,
):
    err = (e0, e1, e2)
    layer = (l0, l1, l2)
    pairs = (
        (feat_hbm, feat), (e0_hbm, e0), (e1_hbm, e1), (e2_hbm, e2), (wdec_hbm, wdec),
        (pre_hbm, pre), (l0_hbm, l0), (l1_hbm, l1), (l2_hbm, l2),
    )
    loads = [pltpu.make_async_copy(src, dst, isem.at[i]) for i, (src, dst) in enumerate(pairs)]
    for load in loads:
        load.start()
    loads[0].wait()
    feat_t[...] = feat[...].T
    loads[4].wait()
    square = jnp.zeros((1, 1), F32)
    stores = []
    for p in PIECES:
        loads[1 + p].wait()
        width = WIDTHS[p]
        for q in range(4):
            low = q * QUARTER + OFFSETS[p]
            rows = err[p][:, :, :, q].reshape(512, width)
            odec[:, low:low + width] = jnp.dot(
                feat_t[...], rows, preferred_element_type=F32
            ).astype(BF16)
            store = pltpu.make_async_copy(
                odec.at[:, pl.ds(low, width)], wdec_grad.at[:, pl.ds(low, width)], dsem.at[p * 4 + q]
            )
            store.start()
            stores.append(store)
            more = lax.dot_general(
                rows, wdec[:, low:low + width], (((1,), (1,)), ((), ())), preferred_element_type=F32
            )
            if p == 0 and q == 0:
                gfeat[...] = more
            else:
                gfeat[...] += more
            wide = rows.astype(F32)
            bdec_grad[:, low:low + width] = jnp.sum(wide, axis=0, keepdims=True)
            square = square + jnp.sum(jnp.sum(wide * wide, axis=0, keepdims=True), axis=1, keepdims=True)
    loss[...] = (0.5 * square + sparsity_coef * gate_in[0:1, 0:1]) / (512 * D)
    loads[5].wait()
    pre_act = pre[...]
    soft = jax.nn.sigmoid((pre_act - threshold[...]) / gate_band)
    slope = soft * (1.0 - soft) / gate_band
    grad_feat = gfeat[...]
    side = (grad_feat * pre_act + sparsity_coef) * slope
    grad_pre = grad_feat * soft + side
    thresh_grad[...] = -jnp.sum(side, axis=0, keepdims=True)
    benc_grad[...] = jnp.sum(grad_pre, axis=0, keepdims=True)
    gpre[...] = grad_pre.astype(BF16)
    for p in PIECES:
        loads[6 + p].wait()
        width = WIDTHS[p]
        for q in range(4):
            low = q * QUARTER + OFFSETS[p]
            rows = layer[p][:, :, :, q].reshape(512, width)
            oenc[low:low + width, :] = lax.dot_general(
                rows, gpre[...], (((0,), (0,)), ((), ())), preferred_element_type=F32
            ).astype(BF16)
            store = pltpu.make_async_copy(
                oenc.at[pl.ds(low, width), :], wenc_grad.at[pl.ds(low, width), :], esem.at[p * 4 + q]
            )
            store.start()
            stores.append(store)
    for store in stores:
        store.wait()


def blocks(dtype=BF16, lead=(2, 4, 4, 4)):
    return [pltpu.VMEM(lead + (16, w), dtype) for w in WIDTHS]


def local(
    residual_in, pre_gain, post_gain, w_gate, w_up, w_down, w_enc, b_enc, threshold, w_dec, b_dec
):
    vmem = pl.BlockSpec(memory_space=pltpu.VMEM)
    hbm = pl.BlockSpec(memory_space=pl.ANY)
    dma = pltpu.SemaphoreType.DMA
    shape = jax.ShapeDtypeStruct
    full = [shape((2, 4, 4, 4, 16, w), BF16) for w in WIDTHS]
    b_enc = b_enc.reshape(1, 512)
    threshold = threshold.reshape(1, 512)
    made = pl.pallas_call(
        mlp_and_sae,
        out_shape=full + full + [
            shape((512, 512), BF16), shape((512, 512), F32), shape((8, 128), F32),
        ],
        in_specs=[vmem] * 6 + [hbm] * 5,
        out_specs=[hbm] * 8 + [vmem],
        scratch_shapes=[
            pltpu.VMEM((448, D), BF16), pltpu.VMEM((448, D), BF16), pltpu.VMEM((448, D), BF16),
            pltpu.VMEM((D, 512), BF16), pltpu.VMEM((512, D), BF16),
            pltpu.VMEM((4, 4, 2, 112, 128), BF16), pltpu.VMEM((D, 128), BF16),
            pltpu.VMEM((128, 448), BF16),
            pltpu.VMEM((2, 4, 4, 16, QUARTER), BF16), pltpu.VMEM((4, 4, 16, QUARTER), BF16),
            pltpu.VMEM((4, 4, 16, QUARTER), BF16), pltpu.VMEM((15, 16, QUARTER), BF16),
            pltpu.VMEM((16, 128), F32), pltpu.VMEM((3, 16, 128), F32),
            *blocks(), pltpu.VMEM((512, 512), BF16), pltpu.VMEM((512, 512), F32),
            *blocks(), *blocks(lead=(4, 4, 4)), *blocks(lead=(4, 4, 4)),
            *blocks(lead=(3, 4, 4)), *blocks(lead=(4, 4)),
            *blocks(lead=(3, 4)), *blocks(lead=(4,)), *blocks(lead=(3,)),
            *blocks(), pltpu.VMEM((4, 8, 128), F32), pltpu.VMEM((10, 8, 128), F32),
            dma((5,)), dma((16,)), dma((16,)), dma((4,)), dma((4,)), dma((15,)), dma((15,)),
            dma((3,)), dma((3,)), dma((3, 3, 3)), dma((3, 3, 3)), dma((3, 4)), dma((3, 4)),
            dma((3,)), dma((3,)), dma((3, 3, 3)), dma((3, 3, 3)),
            dma((3, 3, 3)), dma((3, 3, 3)), dma((3, 4)), dma((3, 4)), dma((10,)), dma((10,)),
            dma((8,)),
        ],
        compiler_params=pltpu.CompilerParams(
            collective_id=0, has_side_effects=True, vmem_limit_bytes=56 * 1024 * 1024
        ),
        name="forward",
    )(
        residual_in.T, pre_gain.reshape(28, 128), post_gain.reshape(28, 128), b_dec.reshape(28, 128),
        b_enc, threshold, w_gate.T, w_up.T, w_down, w_enc, w_dec,
    )
    gate_total = made[8]
    grads = pl.pallas_call(
        gradients,
        out_shape=[
            shape((D, 512), BF16), shape((512, D), BF16), shape((1, 512), F32),
            shape((1, 512), F32), shape((1, D), F32), shape((1, 1), F32),
        ],
        in_specs=[vmem, vmem] + [hbm] * 9,
        out_specs=[hbm, hbm] + [vmem] * 4,
        scratch_shapes=[
            *blocks(), *blocks(), pltpu.VMEM((512, 512), BF16), pltpu.VMEM((512, 512), BF16),
            pltpu.VMEM((512, 512), F32), pltpu.VMEM((512, D), BF16), pltpu.VMEM((512, 512), F32),
            pltpu.VMEM((512, 512), BF16), pltpu.VMEM((512, D), BF16), pltpu.VMEM((D, 512), BF16),
            dma((9,)), dma((12,)), dma((12,)),
        ],
        compiler_params=pltpu.CompilerParams(vmem_limit_bytes=56 * 1024 * 1024),
        name="gradients",
    )(threshold, gate_total, *made[:8], w_dec)
    return (
        grads[5].reshape(()), grads[0], grads[1], grads[2].reshape(512), grads[3].reshape(512),
        grads[4].reshape(D),
    )


def solution(mesh):
    placed = (
        P("dp", "mp"),
        P(),
        P(),
        P(None, "mp"),
        P(None, "mp"),
        P("mp", None),
        P(None, ("dp", "mp")),
        P(("dp", "mp")),
        P(("dp", "mp")),
        P(("dp", "mp"), None),
        P(),
    )
    return jax.shard_map(
        local,
        mesh=mesh,
        in_specs=placed,
        out_specs=(
            P(),
            P(None, ("dp", "mp")),
            P(("dp", "mp"), None),
            P(("dp", "mp")),
            P(("dp", "mp")),
            P(),
        ),
        check_vma=False,
    )
```

```python
import jax
import jax.numpy as jnp
from jax import lax
from jax.experimental import pallas as pl
from jax.experimental.pallas import tpu as pltpu
from jax.sharding import PartitionSpec as P

norm_eps = 1e-06
gate_band = 0.1
sparsity_coef = 0.05

MESH = pl.DeviceIdType.MESH
F32 = jnp.float32
BF16 = jnp.bfloat16

D = 3584
QUARTER = 896
WIDTHS = (256, 256, 384)
OFFSETS = (0, 256, 512)
ORDERS = ("xyz", "yzx", "zxy")
PIECES = (0, 1, 2)


def coordinates():
    y = lax.axis_index("dp")
    m = lax.axis_index("mp")
    return {"x": m // 8, "y": y, "z": (m // 2) % 4, "c": m % 2}


def device(at):
    return (at["y"], (at["x"] * 4 + at["z"]) * 2 + at["c"])


def moved(at, axis, steps):
    there = dict(at)
    there[axis] = (at[axis] + steps) % (2 if axis == "c" else 4)
    return there


def grid_index(at, gathered):
    return tuple(slice(None) if a in gathered else at[a] for a in "yxz")


def halves(at, order, value, half):
    there = dict(at)
    there[order[2]] = value
    first = [a for a in "yxz" if a != order[2]][0]
    return tuple(
        there[a] if a == order[2] else slice(2 * half, 2 * half + 2) if a == first else slice(None)
        for a in "yxz"
    )


def forward(
    resid, pre_gain, post_gain, b_dec, b_enc, threshold,
    wg_hbm, wu_hbm, wd_hbm, we_hbm, wdec_hbm,
    err_out, lt_out, featt_out, gpre_out, gate_out, benc_out, thresh_out,
    wg, wu, wd, we, wdec, gath, norm_t, hidden, bp, bp_in, bs, b_in, sq, sq_in,
    l0, l1, l2, feat, feat_t, pre, soft_s, slope_s, gfeat, gpre, lt,
    p0, p1, p2, pin0, pin1, pin2, s0, s1, s2,
    ra0, ra1, ra2, rl0, rl1, rl2, ro0, ro1, ro2, sa0, sa1, sa2, rb0, rb1, rb2, sb0, sb1, sb2,
    rc0, rc1, rc2, e0, e1, e2, gsum, gin,
    wsem, asend, arecv, bcsend, bcrecv, bsend, brecv, sqsend, sqrecv,
    dsend, drecv, dlsend, dlrecv, dcsend, dcrecv, pcsend, pcrecv, fsend, frecv, rsend, rrecv,
    esend, erecv, elsend, elrecv, ecsend, ecrecv, gsend, grecv, osem,
):
    at = coordinates()
    x, y, z, c = at["x"], at["y"], at["z"], at["c"]
    sibling = device(moved(at, "c", 1))
    layer = (l0, l1, l2)
    part = (p0, p1, p2)
    part_in = (pin0, pin1, pin2)
    total = (s0, s1, s2)
    in_a, relay_in, relay_out, sum_a = (ra0, ra1, ra2), (rl0, rl1, rl2), (ro0, ro1, ro2), (sa0, sa1, sa2)
    in_b, sum_b = (rb0, rb1, rb2), (sb0, sb1, sb2)
    in_c = (rc0, rc1, rc2)
    err = (e0, e1, e2)

    loads = [
        pltpu.make_async_copy(src, dst, wsem.at[i])
        for i, (src, dst) in enumerate(
            ((wg_hbm, wg), (wu_hbm, wu), (wd_hbm, wd), (we_hbm, we), (wdec_hbm, wdec))
        )
    ]

    plane = [(i, j) for i in range(4) for j in range(4) if i or j]
    barrier = pltpu.get_barrier_semaphore()
    greeted = [moved(moved(at, "x", i), "z", j) for i, j in plane]
    greeted += [moved(at, "y", k) for k in (1, 2, 3)] + [moved(at, "c", 1)]
    for there in greeted:
        pl.semaphore_signal(barrier, inc=1, device_id=device(there), device_id_type=MESH)
    pl.semaphore_wait(barrier, len(greeted))

    unsent = []

    def remote(src, dst, send, recv, there):
        copy = pltpu.make_async_remote_copy(
            src_ref=src, dst_ref=dst, send_sem=send, recv_sem=recv,
            device_id=there, device_id_type=MESH,
        )
        copy.start()
        unsent.append(copy)
        return copy

    copies = []
    for n, (i, j) in enumerate(plane):
        there = moved(moved(at, "x", i), "z", j)
        copies.append(remote(resid, gath.at[x, z, c], asend.at[n], arecv.at[n], device(there)))
    loads[0].start()
    loads[1].start()
    gath[x, z, c] = resid[...]
    for copy in copies:
        copy.wait_recv()
    copy = remote(gath.at[:, :, c], gath.at[:, :, c], asend.at[15], arecv.at[15], sibling)
    loads[2].start()
    copy.wait_recv()

    squares = jnp.zeros((1, 128), F32)
    for i in range(4):
        for j in range(4):
            rows = gath[i, j].astype(F32).reshape(224, 128)
            squares = squares + jnp.sum(rows * rows, axis=0, keepdims=True)
    scale = lax.rsqrt(squares / D + norm_eps)
    gains = jnp.concatenate([pre_gain[...], jnp.zeros((100, 128), F32)], axis=0).T
    everything = gath[...].reshape(D, 128)
    for k in range(28):
        rows = everything[k * 128:(k + 1) * 128].astype(F32)
        norm_t[k * 128:(k + 1) * 128, :] = (rows * scale * gains[:, k:k + 1]).astype(BF16)

    loads[0].wait()
    loads[1].wait()
    gate = jnp.dot(wg[...], norm_t[...], preferred_element_type=F32)
    up = jnp.dot(wu[...], norm_t[...], preferred_element_type=F32)
    hidden[...] = (jax.nn.gelu(gate, approximate=True) * up).T.astype(BF16)

    loads[2].wait()
    copies = []
    for q in range(4):
        own = jnp.dot(hidden[...], wd[:, q * QUARTER:(q + 1) * QUARTER], preferred_element_type=F32)
        bp[:, :, q] = own.reshape(2, 4, 16, QUARTER)
        copies.append(remote(bp.at[1 - c, :, q], bp_in.at[:, q], bcsend.at[q], bcrecv.at[q], sibling))
    for q, copy in enumerate(copies):
        copy.wait_recv()
        bs[:, q] = (bp[c, :, q] + bp_in[:, q]).astype(BF16)
    copies = []
    for n, (i, j) in enumerate(plane):
        there = moved(moved(at, "x", i), "z", j)
        copies.append(
            remote(bs.at[there["x"], there["z"]], b_in.at[n], bsend.at[n], brecv.at[n], device(there))
        )
    loads[3].start()
    pick = lax.broadcasted_iota(jnp.int32, (16, 128), 0) + (c * 64 + x * 16)
    pick = (lax.broadcasted_iota(jnp.int32, (16, 128), 1) == pick).astype(BF16)
    mine = lax.dot_general(
        pick, own_rows(gath, z), (((1,), (1,)), ((), ())), preferred_element_type=F32
    )
    block = bp[c, x, z] + bp_in[x, z]
    for n, copy in enumerate(copies):
        copy.wait_recv()
        block = block + b_in[n].astype(F32)
    sums = jnp.broadcast_to(jnp.sum(block * block, axis=1, keepdims=True), (16, 128))
    sq[...] = sums
    copies = [
        remote(sq, sq_in.at[k - 1], sqsend.at[k - 1], sqrecv.at[k - 1], device(moved(at, "z", k)))
        for k in (1, 2, 3)
    ]
    for k, copy in enumerate(copies):
        copy.wait_recv()
        sums = sums + sq_in[k]
    row_scale = lax.rsqrt(sums[:, :1] / D + norm_eps)
    gain = lane_row(post_gain, z)
    block = mine + block * row_scale * gain
    for p in PIECES:
        layer[p][c, y, x, z] = block[:, OFFSETS[p]:OFFSETS[p] + WIDTHS[p]].astype(BF16)

    def gather(arrays, send, recv, lsend, lrecv, csend, crecv, use):
        stage, last, across = {}, {}, {}
        for step in range(2):
            for p in PIECES:
                order = ORDERS[p]
                if step:
                    for copy in stage[p]:
                        copy.wait_recv()
                here = arrays[p].at[(c,) + grid_index(at, order[:step])]
                stage[p] = [
                    remote(here, here, send.at[step, p, k - 1], recv.at[step, p, k - 1],
                           device(moved(at, order[step], k)))
                    for k in (1, 2, 3)
                ]

        def pass_on(p, owner, half, steps, n):
            order = ORDERS[p]
            value = moved(at, order[2], owner)[order[2]]
            ref = arrays[p].at[(c,) + halves(at, order, value, half)]
            return remote(ref, ref, lsend.at[p, n], lrecv.at[p, n], device(moved(at, order[2], steps)))

        def cross(p, owner):
            ref = arrays[p].at[(c,) + grid_index(moved(at, ORDERS[p][2], owner), ORDERS[p][:2])]
            across[p].append(remote(ref, ref, csend.at[p, owner], crecv.at[p, owner], sibling))

        for p in PIECES:
            for copy in stage[p]:
                copy.wait_recv()
            last[p] = [
                pass_on(p, 0, 0, 1, 0), pass_on(p, 0, 1, 3, 1),
                pass_on(p, 0, 1, 1, 2), pass_on(p, 0, 0, 3, 3),
            ]
            across[p] = []
            cross(p, 0)
        for p in PIECES:
            last[p][0].wait_recv()
            last[p].append(pass_on(p, 3, 0, 1, 4))
            last[p][1].wait_recv()
            last[p].append(pass_on(p, 1, 1, 3, 5))
        for p in PIECES:
            last[p][2].wait_recv()
            cross(p, 3)
            last[p][3].wait_recv()
            cross(p, 1)

        def finish(p):
            last[p][4].wait_recv()
            last[p][5].wait_recv()
            cross(p, 2)

        def use_all(p):
            for copy in across[p]:
                copy.wait_recv()
            use(p)

        finish(0)
        finish(1)
        use_all(0)
        finish(2)
        use_all(1)
        use_all(2)

    def encode(p):
        for q in range(4):
            low = q * QUARTER + OFFSETS[p]
            rows = layer[p][:, :, :, q].reshape(512, WIDTHS[p])
            more = jnp.dot(rows, we[low:low + WIDTHS[p], :], preferred_element_type=F32)
            if p == 0 and q == 0:
                pre[...] = b_enc[...] + more
            else:
                pre[...] += more

    loads[3].wait()
    loads[4].start()
    gather(layer, dsend, drecv, dlsend, dlrecv, dcsend, dcrecv, encode)

    pre_act = pre[...]
    soft = jax.nn.sigmoid((pre_act - threshold[...]) / gate_band)
    soft_s[...] = soft
    feat[...] = (pre_act * soft).astype(BF16)

    loads[4].wait()

    def partial(p, half):
        rows = feat[pl.ds(pl.multiple_of(half * 256, 256), 256), :]
        for q in range(4):
            low = q * QUARTER + OFFSETS[p]
            value = jnp.dot(rows, wdec[:, low:low + WIDTHS[p]], preferred_element_type=F32)
            part[p][half, :, :, q] = value.astype(BF16).reshape(4, 4, 16, WIDTHS[p])

    copies = []
    for p in PIECES:
        partial(p, 1 - c)
        copies.append(remote(part[p].at[1 - c], part_in[p], pcsend.at[p], pcrecv.at[p], sibling))
    stage = {}
    for p in PIECES:
        partial(p, c)
        copies[p].wait_recv()
        for i in range(4):
            total[p][i] = (part[p][c, i].astype(F32) + part_in[p][i].astype(F32)).astype(BF16)
        order = ORDERS[p]
        up, down = device(moved(at, order[2], 1)), device(moved(at, order[2], 3))
        value = {k: moved(at, order[2], k)[order[2]] for k in range(4)}

        def piece(k, half):
            return total[p].at[halves(at, order, value[k], half)]

        def first(src, dst, n, there):
            return remote(src, dst, fsend.at[p, n], frecv.at[p, n], there)

        stage[p] = [
            first(piece(2, 0), relay_in[p].at[0], 0, up),
            first(piece(2, 1), relay_in[p].at[1], 1, down),
            first(piece(1, 1), in_a[p].at[0, 2:4], 2, up),
            first(piece(3, 0), in_a[p].at[1, 0:2], 3, down),
        ]
    soft = soft_s[...]
    gate_sum = jnp.broadcast_to(jnp.sum(soft).reshape(1, 1), (8, 128))
    gsum[0] = gate_sum
    gate_copies = [remote(gsum.at[0], gin.at[9], gsend.at[9], grecv.at[9], sibling)]
    for p in PIECES:
        order = ORDERS[p]
        up, down = moved(at, order[2], 1), moved(at, order[2], 3)
        for n, (there, half) in enumerate(((up, 0), (down, 1))):
            stage[p][n].wait_recv()
            own = total[p][halves(at, order, there[order[2]], half)].astype(F32)
            relay_out[p][n] = (own + relay_in[p][n].astype(F32)).astype(BF16)
            stage[p].append(
                remote(relay_out[p].at[n], in_a[p].at[n, 2 * half:2 * half + 2],
                       fsend.at[p, 4 + n], frecv.at[p, 4 + n], device(there))
            )

    gate_copies[0].wait_recv()
    gate_sum = gate_sum + gin[9]

    def gate_step(s, axis, value):
        gsum[1 + s] = value
        return [
            remote(gsum.at[1 + s], gin.at[3 * s + k - 1], gsend.at[3 * s + k - 1],
                   grecv.at[3 * s + k - 1], device(moved(at, axis, k)))
            for k in (1, 2, 3)
        ]

    def gate_finish(s, made, value):
        for k, copy in enumerate(made):
            copy.wait_recv()
            value = value + gin[3 * s + k]
        return value

    gate_copies = gate_step(0, "x", gate_sum)
    slope_s[...] = soft * (1.0 - soft) / gate_band
    feat_t[...] = feat[...].T
    outs = [pltpu.make_async_copy(feat_t, featt_out, osem.at[0])]
    outs[0].start()
    for p in PIECES:
        for q in range(4):
            low = q * QUARTER + OFFSETS[p]
            lt[low:low + WIDTHS[p], :] = layer[p][:, :, :, q].reshape(512, WIDTHS[p]).T
    outs.append(pltpu.make_async_copy(lt, lt_out, osem.at[14]))
    outs[1].start()
    for p in PIECES:
        last, second = ORDERS[p][2], ORDERS[p][1]
        for copy in stage[p][2:]:
            copy.wait_recv()
        value = total[p][grid_index(at, [a for a in "xyz" if a != last])].astype(F32)
        for k in range(2):
            value = value + in_a[p][k].astype(F32)
        sum_a[p][...] = value.astype(BF16)
        stage[p] = []
        left = [a for a in "yxz" if a != last]
        for k in (1, 2, 3):
            there = moved(at, second, k)
            src = sum_a[p].at[tuple(there[a] if a == second else slice(None) for a in left)]
            stage[p].append(
                remote(src, in_b[p].at[k - 1], rsend.at[0, p, k - 1], rrecv.at[0, p, k - 1], device(there))
            )
    gate_sum = gate_finish(0, gate_copies, gate_sum)
    gate_copies = gate_step(1, "y", gate_sum)
    for p in PIECES:
        last, second, first = ORDERS[p][2], ORDERS[p][1], ORDERS[p][0]
        for copy in stage[p]:
            copy.wait_recv()
        left = [a for a in "yxz" if a != last]
        value = sum_a[p][tuple(at[a] if a == second else slice(None) for a in left)].astype(F32)
        for k in range(3):
            value = value + in_b[p][k].astype(F32)
        sum_b[p][...] = value.astype(BF16)
        stage[p] = []
        for k in (1, 2, 3):
            there = moved(at, first, k)
            stage[p].append(
                remote(sum_b[p].at[there[first]], in_c[p].at[k - 1], rsend.at[1, p, k - 1],
                       rrecv.at[1, p, k - 1], device(there))
            )
    gate_sum = gate_finish(1, gate_copies, gate_sum)
    gate_copies = gate_step(2, "z", gate_sum)
    bias = lane_row(b_dec, z)
    for p in PIECES:
        for copy in stage[p]:
            copy.wait_recv()
        value = sum_b[p][at[ORDERS[p][0]]].astype(F32)
        for k in range(3):
            value = value + in_c[p][k].astype(F32)
        value = value + bias[:, OFFSETS[p]:OFFSETS[p] + WIDTHS[p]]
        value = value - layer[p][c, y, x, z].astype(F32)
        err[p][c, y, x, z] = value.astype(BF16)

    def back(p):
        for q in range(4):
            low = q * QUARTER + OFFSETS[p]
            out = pltpu.make_async_copy(
                err[p].at[:, :, :, q], err_out.at[:, :, :, :, low:low + WIDTHS[p]],
                osem.at[1 + 4 * p + q],
            )
            out.start()
            outs.append(out)
        for q in range(4):
            low = q * QUARTER + OFFSETS[p]
            more = lax.dot_general(
                err[p][:, :, :, q].reshape(512, WIDTHS[p]), wdec[:, low:low + WIDTHS[p]],
                (((1,), (1,)), ((), ())), preferred_element_type=F32,
            )
            if p == 0 and q == 0:
                gfeat[...] = more
            else:
                gfeat[...] += more

    gather(err, esend, erecv, elsend, elrecv, ecsend, ecrecv, back)
    gate_out[...] = gate_finish(2, gate_copies, gate_sum)
    grad_feat = gfeat[...]
    side = (grad_feat * pre[...] + sparsity_coef) * slope_s[...]
    grad_pre = grad_feat * soft_s[...] + side
    thresh_out[...] = -jnp.sum(side, axis=0, keepdims=True)
    benc_out[...] = jnp.sum(grad_pre, axis=0, keepdims=True)
    gpre[...] = grad_pre.astype(BF16)
    outs.append(pltpu.make_async_copy(gpre, gpre_out, osem.at[13]))
    outs[-1].start()
    for copy in unsent:
        copy.wait_send()
    for out in outs:
        out.wait()


def own_rows(gath, z):
    return gath[pl.ds(z, 1)].reshape(QUARTER, 128)


def lane_row(ref, z):
    rows = [ref[pl.ds(z * 7 + i, 1), :] for i in range(7)]
    return jnp.concatenate(rows, axis=1)


def gradients(featt, gpre, gate_in, benc, thresh, err, lt, wdec_grad, wenc_grad, bdec_grad, loss,
              benc_grad, thresh_grad, square):
    step = pl.program_id(0)
    rows = err[...]
    wdec_grad[...] = jnp.dot(featt[...], rows, preferred_element_type=F32).astype(BF16)
    wenc_grad[...] = jnp.dot(lt[...], gpre[...], preferred_element_type=F32).astype(BF16)
    wide = rows.astype(F32)
    bdec_grad[...] = jnp.sum(wide, axis=0, keepdims=True)
    more = jnp.sum(wide * wide, axis=0, keepdims=True)

    @pl.when(step == 0)
    def _():
        square[...] = more
        benc_grad[...] = benc[...]
        thresh_grad[...] = thresh[...]

    @pl.when(step > 0)
    def _():
        square[...] += more

    @pl.when(step == pl.num_programs(0) - 1)
    def _():
        loss[0] = (0.5 * jnp.sum(square[...]) + sparsity_coef * gate_in[0, 0]) / (512 * D)


def blocks(dtype=BF16, lead=(2, 4, 4, 4)):
    return [pltpu.VMEM(lead + (16, w), dtype) for w in WIDTHS]


STEP = 512


def local(
    residual_in, pre_gain, post_gain, w_gate, w_up, w_down, w_enc, b_enc, threshold, w_dec, b_dec
):
    vmem = pl.BlockSpec(memory_space=pltpu.VMEM)
    hbm = pl.BlockSpec(memory_space=pl.ANY)
    dma = pltpu.SemaphoreType.DMA
    shape = jax.ShapeDtypeStruct
    square = lambda dtype: pltpu.VMEM((512, 512), dtype)
    err, lt, featt, gpre, gate_total, benc, thresh = pl.pallas_call(
        forward,
        out_shape=[
            shape((2, 4, 4, 16, D), BF16), shape((D, 512), BF16), shape((512, 512), BF16),
            shape((512, 512), BF16), shape((8, 128), F32), shape((1, 512), F32), shape((1, 512), F32),
        ],
        in_specs=[vmem] * 6 + [hbm] * 5,
        out_specs=[hbm] * 4 + [vmem] * 3,
        scratch_shapes=[
            pltpu.VMEM((448, D), BF16), pltpu.VMEM((448, D), BF16), pltpu.VMEM((448, D), BF16),
            pltpu.VMEM((D, 512), BF16), pltpu.VMEM((512, D), BF16),
            pltpu.VMEM((4, 4, 2, 112, 128), BF16), pltpu.VMEM((D, 128), BF16),
            pltpu.VMEM((128, 448), BF16),
            pltpu.VMEM((2, 4, 4, 16, QUARTER), F32), pltpu.VMEM((4, 4, 16, QUARTER), F32),
            pltpu.VMEM((4, 4, 16, QUARTER), BF16), pltpu.VMEM((15, 16, QUARTER), BF16),
            pltpu.VMEM((16, 128), F32), pltpu.VMEM((3, 16, 128), F32),
            *blocks(), square(BF16), square(BF16), square(F32), square(F32), square(F32), square(F32),
            square(BF16), pltpu.VMEM((D, 512), BF16),
            *blocks(), *blocks(lead=(4, 4, 4)), *blocks(lead=(4, 4, 4)),
            *blocks(lead=(2, 4, 4)), *blocks(lead=(2, 2, 4)), *blocks(lead=(2, 2, 4)),
            *blocks(lead=(4, 4)), *blocks(lead=(3, 4)), *blocks(lead=(4,)), *blocks(lead=(3,)),
            *blocks(), pltpu.VMEM((4, 8, 128), F32), pltpu.VMEM((10, 8, 128), F32),
            dma((5,)), dma((16,)), dma((16,)), dma((4,)), dma((4,)), dma((15,)), dma((15,)),
            dma((3,)), dma((3,)),
            dma((2, 3, 3)), dma((2, 3, 3)), dma((3, 6)), dma((3, 6)), dma((3, 4)), dma((3, 4)),
            dma((3,)), dma((3,)), dma((3, 6)), dma((3, 6)), dma((2, 3, 3)), dma((2, 3, 3)),
            dma((2, 3, 3)), dma((2, 3, 3)), dma((3, 6)), dma((3, 6)), dma((3, 4)), dma((3, 4)),
            dma((10,)), dma((10,)), dma((15,)),
        ],
        compiler_params=pltpu.CompilerParams(
            collective_id=0, has_side_effects=True, vmem_limit_bytes=58 * 1024 * 1024
        ),
        name="forward",
    )(
        residual_in.T, pre_gain.reshape(28, 128), post_gain.reshape(28, 128), b_dec.reshape(28, 128),
        b_enc.reshape(1, 512), threshold.reshape(1, 512), w_gate.T, w_up.T, w_down, w_enc, w_dec,
    )
    fixed = lambda dims: pl.BlockSpec(dims, lambda i: (0, 0))
    across = pl.BlockSpec((512, STEP), lambda i: (0, i))
    along = pl.BlockSpec((STEP, 512), lambda i: (i, 0))
    grads = pl.pallas_call(
        gradients,
        grid=(D // STEP,),
        out_shape=[
            shape((512, D), BF16), shape((D, 512), BF16), shape((1, D), F32), shape((1,), F32),
            shape((1, 512), F32), shape((1, 512), F32),
        ],
        in_specs=[
            fixed((512, 512)), fixed((512, 512)), fixed((8, 128)), fixed((1, 512)), fixed((1, 512)),
            across, along,
        ],
        out_specs=[
            across, along, pl.BlockSpec((1, STEP), lambda i: (0, i)),
            pl.BlockSpec(memory_space=pltpu.SMEM), fixed((1, 512)), fixed((1, 512)),
        ],
        scratch_shapes=[pltpu.VMEM((1, STEP), F32)],
        compiler_params=pltpu.CompilerParams(vmem_limit_bytes=60 * 1024 * 1024),
        name="gradients",
    )(featt, gpre, gate_total, benc, thresh, err.reshape(512, D), lt)
    return (
        grads[3].reshape(()), grads[1], grads[0], grads[4].reshape(512), grads[5].reshape(512),
        grads[2].reshape(D),
    )


def solution(mesh):
    placed = (
        P("dp", "mp"),
        P(),
        P(),
        P(None, "mp"),
        P(None, "mp"),
        P("mp", None),
        P(None, ("dp", "mp")),
        P(("dp", "mp")),
        P(("dp", "mp")),
        P(("dp", "mp"), None),
        P(),
    )
    return jax.shard_map(
        local,
        mesh=mesh,
        in_specs=placed,
        out_specs=(
            P(),
            P(None, ("dp", "mp")),
            P(("dp", "mp"), None),
            P(("dp", "mp")),
            P(("dp", "mp")),
            P(),
        ),
        check_vma=False,
    )
```

```python
import jax
import jax.numpy as jnp
from jax import lax
from jax.experimental import pallas as pl
from jax.experimental.pallas import tpu as pltpu
from jax.sharding import PartitionSpec as P

norm_eps = 1e-06
gate_band = 0.1
sparsity_coef = 0.05

MESH = pl.DeviceIdType.MESH
F32 = jnp.float32
BF16 = jnp.bfloat16

D = 3584
QUARTER = 896
WIDTHS = (256, 256, 384)
OFFSETS = (0, 256, 512)
ORDERS = ("xyz", "yzx", "zxy")
PIECES = (0, 1, 2)


def coordinates():
    y = lax.axis_index("dp")
    m = lax.axis_index("mp")
    return {"x": m // 8, "y": y, "z": (m // 2) % 4, "c": m % 2}


def device(at):
    return (at["y"], (at["x"] * 4 + at["z"]) * 2 + at["c"])


def moved(at, axis, steps):
    there = dict(at)
    there[axis] = (at[axis] + steps) % (2 if axis == "c" else 4)
    return there


def grid_index(at, gathered):
    return tuple(slice(None) if a in gathered else at[a] for a in "yxz")


def halves(at, order, value, half):
    there = dict(at)
    there[order[2]] = value
    first = [a for a in "yxz" if a != order[2]][0]
    return tuple(
        there[a] if a == order[2] else slice(2 * half, 2 * half + 2) if a == first else slice(None)
        for a in "yxz"
    )


def forward(
    resid, pre_gain_hbm, post_gain_hbm, b_dec_hbm, b_enc_hbm, threshold_hbm,
    wg_hbm, wu_hbm, wd_hbm, we_hbm, wdec_hbm,
    err_out, lt_out, featt_out, gpre_out, gate_out, benc_out, thresh_out,
    pre_gain, post_gain, b_dec, b_enc, threshold, wg, wu, wd, we, wdec, gath, norm_t, hidden, bp, bp_in, bs, b_in, sq, sq_in,
    l0, l1, l2, feat, feat_t, pre, soft_s, slope_s, gfeat, gpre, lt,
    p0, p1, p2, pin0, pin1, pin2, s0, s1, s2,
    ra0, ra1, ra2, rl0, rl1, rl2, ro0, ro1, ro2, sa0, sa1, sa2, rb0, rb1, rb2, sb0, sb1, sb2,
    rc0, rc1, rc2, e0, e1, e2, gsum, gin,
    wsem, asend, arecv, bcsend, bcrecv, bsend, brecv, sqsend, sqrecv,
    dsend, drecv, dlsend, dlrecv, dcsend, dcrecv, pcsend, pcrecv, fsend, frecv, rsend, rrecv,
    esend, erecv, elsend, elrecv, ecsend, ecrecv, gsend, grecv, osem,
):
    at = coordinates()
    x, y, z, c = at["x"], at["y"], at["z"], at["c"]
    sibling = device(moved(at, "c", 1))
    layer = (l0, l1, l2)
    part = (p0, p1, p2)
    part_in = (pin0, pin1, pin2)
    total = (s0, s1, s2)
    in_a, relay_in, relay_out, sum_a = (ra0, ra1, ra2), (rl0, rl1, rl2), (ro0, ro1, ro2), (sa0, sa1, sa2)
    in_b, sum_b = (rb0, rb1, rb2), (sb0, sb1, sb2)
    in_c = (rc0, rc1, rc2)
    err = (e0, e1, e2)

    loads = [
        pltpu.make_async_copy(src, dst, wsem.at[i])
        for i, (src, dst) in enumerate(
            ((wg_hbm, wg), (wu_hbm, wu), (wd_hbm, wd), (we_hbm, we), (wdec_hbm, wdec),
             (pre_gain_hbm, pre_gain), (post_gain_hbm, post_gain), (b_dec_hbm, b_dec),
             (b_enc_hbm, b_enc), (threshold_hbm, threshold),
             (resid, gath.at[at["x"], at["z"], at["c"]]))
        )
    ]
    for load in loads[5:]:
        load.start()

    plane = [(i, j) for i in range(4) for j in range(4) if i or j]
    barrier = pltpu.get_barrier_semaphore()
    greeted = [moved(moved(at, "x", i), "z", j) for i, j in plane]
    greeted += [moved(at, "y", k) for k in (1, 2, 3)] + [moved(at, "c", 1)]
    for there in greeted:
        pl.semaphore_signal(barrier, inc=1, device_id=device(there), device_id_type=MESH)
    pl.semaphore_wait(barrier, len(greeted))

    unsent = []

    def remote(src, dst, send, recv, there):
        copy = pltpu.make_async_remote_copy(
            src_ref=src, dst_ref=dst, send_sem=send, recv_sem=recv,
            device_id=there, device_id_type=MESH,
        )
        copy.start()
        unsent.append(copy)
        return copy

    copies = []
    for n, (i, j) in enumerate(plane):
        there = moved(moved(at, "x", i), "z", j)
        copies.append(remote(resid, gath.at[x, z, c], asend.at[n], arecv.at[n], device(there)))
    loads[0].start()
    loads[1].start()
    for load in loads[5:]:
        load.wait()
    for copy in copies:
        copy.wait_recv()
    copy = remote(gath.at[:, :, c], gath.at[:, :, c], asend.at[15], arecv.at[15], sibling)
    loads[2].start()
    copy.wait_recv()

    squares = jnp.zeros((1, 128), F32)
    for i in range(4):
        for j in range(4):
            rows = gath[i, j].astype(F32).reshape(224, 128)
            squares = squares + jnp.sum(rows * rows, axis=0, keepdims=True)
    scale = lax.rsqrt(squares / D + norm_eps)
    gains = jnp.concatenate([pre_gain[...], jnp.zeros((100, 128), F32)], axis=0).T
    everything = gath[...].reshape(D, 128)
    for k in range(28):
        rows = everything[k * 128:(k + 1) * 128].astype(F32)
        norm_t[k * 128:(k + 1) * 128, :] = (rows * scale * gains[:, k:k + 1]).astype(BF16)

    loads[0].wait()
    loads[1].wait()
    gate = jnp.dot(wg[...], norm_t[...], preferred_element_type=F32)
    up = jnp.dot(wu[...], norm_t[...], preferred_element_type=F32)
    hidden[...] = (jax.nn.gelu(gate, approximate=True) * up).T.astype(BF16)

    loads[2].wait()
    copies = []
    for q in range(4):
        own = jnp.dot(hidden[...], wd[:, q * QUARTER:(q + 1) * QUARTER], preferred_element_type=F32)
        bp[:, :, q] = own.reshape(2, 4, 16, QUARTER)
        copies.append(remote(bp.at[1 - c, :, q], bp_in.at[:, q], bcsend.at[q], bcrecv.at[q], sibling))
    for q, copy in enumerate(copies):
        copy.wait_recv()
        bs[:, q] = (bp[c, :, q] + bp_in[:, q]).astype(BF16)
    copies = []
    for n, (i, j) in enumerate(plane):
        there = moved(moved(at, "x", i), "z", j)
        copies.append(
            remote(bs.at[there["x"], there["z"]], b_in.at[n], bsend.at[n], brecv.at[n], device(there))
        )
    loads[3].start()
    pick = lax.broadcasted_iota(jnp.int32, (16, 128), 0) + (c * 64 + x * 16)
    pick = (lax.broadcasted_iota(jnp.int32, (16, 128), 1) == pick).astype(BF16)
    mine = lax.dot_general(
        pick, own_rows(gath, z), (((1,), (1,)), ((), ())), preferred_element_type=F32
    )
    block = bp[c, x, z] + bp_in[x, z]
    for n, copy in enumerate(copies):
        copy.wait_recv()
        block = block + b_in[n].astype(F32)
    sums = jnp.broadcast_to(jnp.sum(block * block, axis=1, keepdims=True), (16, 128))
    sq[...] = sums
    copies = [
        remote(sq, sq_in.at[k - 1], sqsend.at[k - 1], sqrecv.at[k - 1], device(moved(at, "z", k)))
        for k in (1, 2, 3)
    ]
    for k, copy in enumerate(copies):
        copy.wait_recv()
        sums = sums + sq_in[k]
    row_scale = lax.rsqrt(sums[:, :1] / D + norm_eps)
    gain = lane_row(post_gain, z)
    block = mine + block * row_scale * gain
    for p in PIECES:
        layer[p][c, y, x, z] = block[:, OFFSETS[p]:OFFSETS[p] + WIDTHS[p]].astype(BF16)

    def gather(arrays, send, recv, lsend, lrecv, csend, crecv, use, known=0):
        stage, last, across = {}, {}, {}
        for step in range(known, 2):
            for p in PIECES:
                order = ORDERS[p]
                if step > known:
                    for copy in stage[p]:
                        copy.wait_recv()
                here = arrays[p].at[(c,) + grid_index(at, order[:step])]
                stage[p] = [
                    remote(here, here, send.at[step, p, k - 1], recv.at[step, p, k - 1],
                           device(moved(at, order[step], k)))
                    for k in (1, 2, 3)
                ]

        def pass_on(p, owner, half, steps, n):
            order = ORDERS[p]
            value = moved(at, order[2], owner)[order[2]]
            ref = arrays[p].at[(c,) + halves(at, order, value, half)]
            return remote(ref, ref, lsend.at[p, n], lrecv.at[p, n], device(moved(at, order[2], steps)))

        def cross(p, owner):
            ref = arrays[p].at[(c,) + grid_index(moved(at, ORDERS[p][2], owner), ORDERS[p][:2])]
            across[p].append(remote(ref, ref, csend.at[p, owner], crecv.at[p, owner], sibling))

        for p in PIECES:
            for copy in stage[p]:
                copy.wait_recv()
            last[p] = [
                pass_on(p, 0, 0, 1, 0), pass_on(p, 0, 1, 3, 1),
                pass_on(p, 0, 1, 1, 2), pass_on(p, 0, 0, 3, 3),
            ]
            across[p] = []
            cross(p, 0)
        for p in PIECES:
            last[p][0].wait_recv()
            last[p].append(pass_on(p, 3, 0, 1, 4))
            last[p][1].wait_recv()
            last[p].append(pass_on(p, 1, 1, 3, 5))
        for p in PIECES:
            last[p][2].wait_recv()
            cross(p, 3)
            last[p][3].wait_recv()
            cross(p, 1)

        def finish(p):
            last[p][4].wait_recv()
            last[p][5].wait_recv()
            cross(p, 2)

        finish(0)
        finish(1)
        use(0, c)
        finish(2)
        use(1, c)
        use(2, c)
        for p in PIECES:
            for copy in across[p]:
                copy.wait_recv()
            use(p, 1 - c)

    def encode(p, half):
        tokens = pl.ds(pl.multiple_of(half * 256, 256), 256)
        for q in range(4):
            low = q * QUARTER + OFFSETS[p]
            rows = layer[p][half, :, :, q].reshape(256, WIDTHS[p])
            more = jnp.dot(rows, we[low:low + WIDTHS[p], :], preferred_element_type=F32)
            if p == 0 and q == 0:
                pre[tokens, :] = b_enc[...] + more
            else:
                pre[tokens, :] += more

    loads[3].wait()
    loads[4].start()
    gather(layer, dsend, drecv, dlsend, dlrecv, dcsend, dcrecv, encode)

    pre_act = pre[...]
    soft = jax.nn.sigmoid((pre_act - threshold[...]) / gate_band)
    soft_s[...] = soft
    feat[...] = (pre_act * soft).astype(BF16)

    loads[4].wait()

    def partial(p, half):
        rows = feat[pl.ds(pl.multiple_of(half * 256, 256), 256), :]
        for q in range(4):
            low = q * QUARTER + OFFSETS[p]
            value = jnp.dot(rows, wdec[:, low:low + WIDTHS[p]], preferred_element_type=F32)
            part[p][half, :, :, q] = value.astype(BF16).reshape(4, 4, 16, WIDTHS[p])

    copies = []
    for p in PIECES:
        partial(p, 1 - c)
        copies.append(remote(part[p].at[1 - c], part_in[p], pcsend.at[p], pcrecv.at[p], sibling))
    stage = {}
    for p in PIECES:
        partial(p, c)
        copies[p].wait_recv()
        for i in range(4):
            total[p][i] = (part[p][c, i].astype(F32) + part_in[p][i].astype(F32)).astype(BF16)
        order = ORDERS[p]
        up, down = device(moved(at, order[2], 1)), device(moved(at, order[2], 3))
        value = {k: moved(at, order[2], k)[order[2]] for k in range(4)}

        def piece(k, half):
            return total[p].at[halves(at, order, value[k], half)]

        def first(src, dst, n, there):
            return remote(src, dst, fsend.at[p, n], frecv.at[p, n], there)

        stage[p] = [
            first(piece(2, 0), relay_in[p].at[0], 0, up),
            first(piece(2, 1), relay_in[p].at[1], 1, down),
            first(piece(1, 1), in_a[p].at[0, 2:4], 2, up),
            first(piece(3, 0), in_a[p].at[1, 0:2], 3, down),
        ]
    soft = soft_s[...]
    gate_sum = jnp.broadcast_to(jnp.sum(soft).reshape(1, 1), (8, 128))
    gsum[0] = gate_sum
    gate_copies = [remote(gsum.at[0], gin.at[9], gsend.at[9], grecv.at[9], sibling)]
    for p in PIECES:
        order = ORDERS[p]
        up, down = moved(at, order[2], 1), moved(at, order[2], 3)
        for n, (there, half) in enumerate(((up, 0), (down, 1))):
            stage[p][n].wait_recv()
            own = total[p][halves(at, order, there[order[2]], half)].astype(F32)
            relay_out[p][n] = (own + relay_in[p][n].astype(F32)).astype(BF16)
            stage[p].append(
                remote(relay_out[p].at[n], in_a[p].at[n, 2 * half:2 * half + 2],
                       fsend.at[p, 4 + n], frecv.at[p, 4 + n], device(there))
            )

    gate_copies[0].wait_recv()
    gate_sum = gate_sum + gin[9]

    def gate_step(s, axis, value):
        gsum[1 + s] = value
        return [
            remote(gsum.at[1 + s], gin.at[3 * s + k - 1], gsend.at[3 * s + k - 1],
                   grecv.at[3 * s + k - 1], device(moved(at, axis, k)))
            for k in (1, 2, 3)
        ]

    def gate_finish(s, made, value):
        for k, copy in enumerate(made):
            copy.wait_recv()
            value = value + gin[3 * s + k]
        return value

    gate_copies = gate_step(0, "x", gate_sum)
    slope_s[...] = soft * (1.0 - soft) / gate_band
    feat_t[...] = feat[...].T
    outs = [pltpu.make_async_copy(feat_t, featt_out, osem.at[0])]
    outs[0].start()
    for p in PIECES:
        for q in range(4):
            low = q * QUARTER + OFFSETS[p]
            lt[low:low + WIDTHS[p], :] = layer[p][:, :, :, q].reshape(512, WIDTHS[p]).T
    outs.append(pltpu.make_async_copy(lt, lt_out, osem.at[1]))
    outs[1].start()
    for p in PIECES:
        last, second = ORDERS[p][2], ORDERS[p][1]
        for copy in stage[p][2:]:
            copy.wait_recv()
        value = total[p][grid_index(at, [a for a in "xyz" if a != last])].astype(F32)
        for k in range(2):
            value = value + in_a[p][k].astype(F32)
        sum_a[p][...] = value.astype(BF16)
        stage[p] = []
        left = [a for a in "yxz" if a != last]
        for k in (1, 2, 3):
            there = moved(at, second, k)
            src = sum_a[p].at[tuple(there[a] if a == second else slice(None) for a in left)]
            stage[p].append(
                remote(src, in_b[p].at[k - 1], rsend.at[0, p, k - 1], rrecv.at[0, p, k - 1], device(there))
            )
    gate_sum = gate_finish(0, gate_copies, gate_sum)
    gate_copies = gate_step(1, "y", gate_sum)
    for p in PIECES:
        last, second, first = ORDERS[p][2], ORDERS[p][1], ORDERS[p][0]
        for copy in stage[p]:
            copy.wait_recv()
        left = [a for a in "yxz" if a != last]
        value = sum_a[p][tuple(at[a] if a == second else slice(None) for a in left)].astype(F32)
        for k in range(3):
            value = value + in_b[p][k].astype(F32)
        value = value.astype(BF16)
        sum_b[p][...] = value
        in_c[p][at[first]] = value
        stage[p] = []
        for k in (1, 2, 3):
            stage[p].append(
                remote(sum_b[p], in_c[p].at[at[first]], rsend.at[1, p, k - 1],
                       rrecv.at[1, p, k - 1], device(moved(at, first, k)))
            )
    gate_sum = gate_finish(1, gate_copies, gate_sum)
    gate_copies = gate_step(2, "z", gate_sum)
    for p in PIECES:
        first = ORDERS[p][0]
        for copy in stage[p]:
            copy.wait_recv()
        for i in range(4):
            value = in_c[p][0, i].astype(F32)
            for k in (1, 2, 3):
                value = value + in_c[p][k, i].astype(F32)
            there = dict(at)
            there[first] = i
            bias = lane_row(b_dec, there["z"])
            value = value + bias[:, OFFSETS[p]:OFFSETS[p] + WIDTHS[p]]
            value = value - layer[p][c, there["y"], there["x"], there["z"]].astype(F32)
            err[p][c, there["y"], there["x"], there["z"]] = value.astype(BF16)

    def back(p, half):
        tokens = pl.ds(pl.multiple_of(half * 256, 256), 256)
        for q in range(4):
            low = q * QUARTER + OFFSETS[p]
            out = pltpu.make_async_copy(
                err[p].at[half, :, :, q], err_out.at[half, :, :, :, low:low + WIDTHS[p]],
                osem.at[len(outs)],
            )
            out.start()
            outs.append(out)
        for q in range(4):
            low = q * QUARTER + OFFSETS[p]
            more = lax.dot_general(
                err[p][half, :, :, q].reshape(256, WIDTHS[p]), wdec[:, low:low + WIDTHS[p]],
                (((1,), (1,)), ((), ())), preferred_element_type=F32,
            )
            if p == 0 and q == 0:
                gfeat[tokens, :] = more
            else:
                gfeat[tokens, :] += more

    gather(err, esend, erecv, elsend, elrecv, ecsend, ecrecv, back, 1)
    gate_out[...] = gate_finish(2, gate_copies, gate_sum)
    grad_feat = gfeat[...]
    side = (grad_feat * pre[...] + sparsity_coef) * slope_s[...]
    grad_pre = grad_feat * soft_s[...] + side
    thresh_out[...] = -jnp.sum(side, axis=0, keepdims=True)
    benc_out[...] = jnp.sum(grad_pre, axis=0, keepdims=True)
    gpre[...] = grad_pre.astype(BF16)
    outs.append(pltpu.make_async_copy(gpre, gpre_out, osem.at[26]))
    outs[-1].start()
    for copy in unsent:
        copy.wait_send()
    for out in outs:
        out.wait()


def own_rows(gath, z):
    return gath[pl.ds(z, 1)].reshape(QUARTER, 128)


def lane_row(ref, z):
    rows = [ref[pl.ds(z * 7 + i, 1), :] for i in range(7)]
    return jnp.concatenate(rows, axis=1)


def gradients(featt, gpre, gate_in, benc, thresh, err, lt, wdec_grad, wenc_grad, bdec_grad, loss,
              benc_grad, thresh_grad, square):
    step = pl.program_id(0)
    rows = err[...]
    wdec_grad[...] = jnp.dot(featt[...], rows, preferred_element_type=F32).astype(BF16)
    wenc_grad[...] = jnp.dot(lt[...], gpre[...], preferred_element_type=F32).astype(BF16)
    wide = rows.astype(F32)
    sums = jnp.sum(wide, axis=0, keepdims=True)
    for i in range(STEP // 128):
        bdec_grad[pl.ds(step * (STEP // 128) + i, 1), :] = sums[:, i * 128:(i + 1) * 128]
    more = jnp.sum(wide * wide, axis=0, keepdims=True)

    @pl.when(step == 0)
    def _():
        square[...] = more
        benc_grad[...] = benc[...]
        thresh_grad[...] = thresh[...]

    @pl.when(step > 0)
    def _():
        square[...] += more

    @pl.when(step == pl.num_programs(0) - 1)
    def _():
        loss[0] = (0.5 * jnp.sum(square[...]) + sparsity_coef * gate_in[0, 0]) / (512 * D)


def blocks(dtype=BF16, lead=(2, 4, 4, 4)):
    return [pltpu.VMEM(lead + (16, w), dtype) for w in WIDTHS]


STEP = 512


def local(
    residual_in, pre_gain, post_gain, w_gate, w_up, w_down, w_enc, b_enc, threshold, w_dec, b_dec
):
    vmem = pl.BlockSpec(memory_space=pltpu.VMEM)
    hbm = pl.BlockSpec(memory_space=pl.ANY)
    dma = pltpu.SemaphoreType.DMA
    shape = jax.ShapeDtypeStruct
    square = lambda dtype: pltpu.VMEM((512, 512), dtype)
    err, lt, featt, gpre, gate_total, benc, thresh = pl.pallas_call(
        forward,
        out_shape=[
            shape((2, 4, 4, 16, D), BF16), shape((D, 512), BF16), shape((512, 512), BF16),
            shape((512, 512), BF16), shape((8, 128), F32), shape((1, 512), F32), shape((1, 512), F32),
        ],
        in_specs=[hbm] * 11,
        out_specs=[hbm] * 4 + [vmem] * 3,
        scratch_shapes=[
            *[pltpu.VMEM((28, 128), F32)] * 3, *[pltpu.VMEM((1, 512), F32)] * 2,
            pltpu.VMEM((448, D), BF16), pltpu.VMEM((448, D), BF16), pltpu.VMEM((448, D), BF16),
            pltpu.VMEM((D, 512), BF16), pltpu.VMEM((512, D), BF16),
            pltpu.VMEM((4, 4, 2, 112, 128), BF16), pltpu.VMEM((D, 128), BF16),
            pltpu.VMEM((128, 448), BF16),
            pltpu.VMEM((2, 4, 4, 16, QUARTER), F32), pltpu.VMEM((4, 4, 16, QUARTER), F32),
            pltpu.VMEM((4, 4, 16, QUARTER), BF16), pltpu.VMEM((15, 16, QUARTER), BF16),
            pltpu.VMEM((16, 128), F32), pltpu.VMEM((3, 16, 128), F32),
            *blocks(), square(BF16), square(BF16), square(F32), square(F32), square(F32), square(F32),
            square(BF16), pltpu.VMEM((D, 512), BF16),
            *blocks(), *blocks(lead=(4, 4, 4)), *blocks(lead=(4, 4, 4)),
            *blocks(lead=(2, 4, 4)), *blocks(lead=(2, 2, 4)), *blocks(lead=(2, 2, 4)),
            *blocks(lead=(4, 4)), *blocks(lead=(3, 4)), *blocks(lead=(4,)), *blocks(lead=(4, 4)),
            *blocks(), pltpu.VMEM((4, 8, 128), F32), pltpu.VMEM((10, 8, 128), F32),
            dma((11,)), dma((16,)), dma((16,)), dma((4,)), dma((4,)), dma((15,)), dma((15,)),
            dma((3,)), dma((3,)),
            dma((2, 3, 3)), dma((2, 3, 3)), dma((3, 6)), dma((3, 6)), dma((3, 4)), dma((3, 4)),
            dma((3,)), dma((3,)), dma((3, 6)), dma((3, 6)), dma((2, 3, 3)), dma((2, 3, 3)),
            dma((2, 3, 3)), dma((2, 3, 3)), dma((3, 6)), dma((3, 6)), dma((3, 4)), dma((3, 4)),
            dma((10,)), dma((10,)), dma((27,)),
        ],
        compiler_params=pltpu.CompilerParams(
            collective_id=0, has_side_effects=True, vmem_limit_bytes=58 * 1024 * 1024
        ),
        name="forward",
    )(
        residual_in.T, pre_gain.reshape(28, 128), post_gain.reshape(28, 128), b_dec.reshape(28, 128),
        b_enc.reshape(1, 512), threshold.reshape(1, 512), w_gate.T, w_up.T, w_down, w_enc, w_dec,
    )
    fixed = lambda dims: pl.BlockSpec(dims, lambda i: (0, 0))
    across = pl.BlockSpec((512, STEP), lambda i: (0, i))
    along = pl.BlockSpec((STEP, 512), lambda i: (i, 0))
    grads = pl.pallas_call(
        gradients,
        grid=(D // STEP,),
        out_shape=[
            shape((512, D), BF16), shape((D, 512), BF16), shape((28, 128), F32), shape((1,), F32),
            shape((1, 512), F32), shape((1, 512), F32),
        ],
        in_specs=[
            fixed((512, 512)), fixed((512, 512)), fixed((8, 128)), fixed((1, 512)), fixed((1, 512)),
            across, along,
        ],
        out_specs=[
            across, along, fixed((28, 128)),
            pl.BlockSpec(memory_space=pltpu.SMEM), fixed((1, 512)), fixed((1, 512)),
        ],
        scratch_shapes=[pltpu.VMEM((1, STEP), F32)],
        compiler_params=pltpu.CompilerParams(vmem_limit_bytes=60 * 1024 * 1024),
        name="gradients",
    )(featt, gpre, gate_total, benc, thresh, err.reshape(512, D), lt)
    return (
        grads[3].reshape(()), grads[1], grads[0], grads[4].reshape(512), grads[5].reshape(512),
        grads[2].reshape(D),
    )


def solution(mesh):
    placed = (
        P("dp", "mp"),
        P(),
        P(),
        P(None, "mp"),
        P(None, "mp"),
        P("mp", None),
        P(None, ("dp", "mp")),
        P(("dp", "mp")),
        P(("dp", "mp")),
        P(("dp", "mp"), None),
        P(),
    )
    return jax.shard_map(
        local,
        mesh=mesh,
        in_specs=placed,
        out_specs=(
            P(),
            P(None, ("dp", "mp")),
            P(("dp", "mp"), None),
            P(("dp", "mp")),
            P(("dp", "mp")),
            P(),
        ),
        check_vma=False,
    )
```

```python
import jax
import jax.numpy as jnp
from jax import lax
from jax.experimental import pallas as pl
from jax.experimental.pallas import tpu as pltpu
from jax.sharding import PartitionSpec as P

norm_eps = 1e-06
gate_band = 0.1
sparsity_coef = 0.05

MESH = pl.DeviceIdType.MESH
F32 = jnp.float32
BF16 = jnp.bfloat16

D = 3584
QUARTER = 896
WIDTHS = (256, 256, 384)
OFFSETS = (0, 256, 512)
ORDERS = ("xyz", "yzx", "zxy")
PIECES = (0, 1, 2)
WIDEST_FIRST = (2, 0, 1)


def coordinates():
    y = lax.axis_index("dp")
    m = lax.axis_index("mp")
    return {"x": m // 8, "y": y, "z": (m // 2) % 4, "c": m % 2}


def device(at):
    return (at["y"], (at["x"] * 4 + at["z"]) * 2 + at["c"])


def moved(at, axis, steps):
    there = dict(at)
    there[axis] = (at[axis] + steps) % (2 if axis == "c" else 4)
    return there


def grid_index(at, gathered):
    return tuple(slice(None) if a in gathered else at[a] for a in "yxz")


def halves(at, order, value, half):
    there = dict(at)
    there[order[2]] = value
    first = [a for a in "yxz" if a != order[2]][0]
    return tuple(
        there[a] if a == order[2] else slice(2 * half, 2 * half + 2) if a == first else slice(None)
        for a in "yxz"
    )


def forward(
    resid, pre_gain_hbm, post_gain_hbm, b_dec_hbm, b_enc_hbm, threshold_hbm,
    wg_hbm, wu_hbm, wd_hbm, we_hbm, wdec_hbm,
    err_out, lt_out, featt_out, gpre_out, gate_out, benc_out, thresh_out,
    pre_gain, post_gain, b_dec, b_enc, threshold, wg, wu, wd, we, wdec, gath, norm_t, hidden, bp, bp_in, bs, b_in, sq, sq_in,
    l0, l1, l2, feat, feat_t, pre, soft_s, slope_s, gfeat, gpre, lt,
    p0, p1, p2, pin0, pin1, pin2, s0, s1, s2,
    ra0, ra1, ra2, rl0, rl1, rl2, ro0, ro1, ro2, sa0, sa1, sa2, rb0, rb1, rb2, sb0, sb1, sb2,
    rc0, rc1, rc2, e0, e1, e2, gsum, gin,
    wsem, asend, arecv, bcsend, bcrecv, bsend, brecv, sqsend, sqrecv,
    dsend, drecv, dlsend, dlrecv, dcsend, dcrecv, pcsend, pcrecv, fsend, frecv, rsend, rrecv,
    esend, erecv, elsend, elrecv, ecsend, ecrecv, gsend, grecv, osem,
):
    at = coordinates()
    x, y, z, c = at["x"], at["y"], at["z"], at["c"]
    sibling = device(moved(at, "c", 1))
    layer = (l0, l1, l2)
    part = (p0, p1, p2)
    part_in = (pin0, pin1, pin2)
    total = (s0, s1, s2)
    in_a, relay_in, relay_out, sum_a = (ra0, ra1, ra2), (rl0, rl1, rl2), (ro0, ro1, ro2), (sa0, sa1, sa2)
    in_b, sum_b = (rb0, rb1, rb2), (sb0, sb1, sb2)
    in_c = (rc0, rc1, rc2)
    err = (e0, e1, e2)

    loads = [
        pltpu.make_async_copy(src, dst, wsem.at[i])
        for i, (src, dst) in enumerate(
            ((wg_hbm, wg), (wu_hbm, wu), (wd_hbm, wd), (we_hbm, we), (wdec_hbm, wdec),
             (pre_gain_hbm, pre_gain), (post_gain_hbm, post_gain), (b_dec_hbm, b_dec),
             (b_enc_hbm, b_enc), (threshold_hbm, threshold),
             (resid, gath.at[at["x"], at["z"], at["c"]]))
        )
    ]
    for load in loads[5:]:
        load.start()

    plane = [(i, j) for i in range(4) for j in range(4) if i or j]
    barrier = pltpu.get_barrier_semaphore()
    greeted = [moved(moved(at, "x", i), "z", j) for i, j in plane]
    greeted += [moved(at, "y", k) for k in (1, 2, 3)] + [moved(at, "c", 1)]
    for there in greeted:
        pl.semaphore_signal(barrier, inc=1, device_id=device(there), device_id_type=MESH)
    pl.semaphore_wait(barrier, len(greeted))

    unsent = []

    def remote(src, dst, send, recv, there):
        copy = pltpu.make_async_remote_copy(
            src_ref=src, dst_ref=dst, send_sem=send, recv_sem=recv,
            device_id=there, device_id_type=MESH,
        )
        copy.start()
        unsent.append(copy)
        return copy

    copies = []
    for n, (i, j) in enumerate(plane):
        there = moved(moved(at, "x", i), "z", j)
        copies.append(remote(resid, gath.at[x, z, c], asend.at[n], arecv.at[n], device(there)))
    loads[0].start()
    loads[1].start()
    for load in loads[5:]:
        load.wait()
    across = []
    for n, i in enumerate((0, 1, 3, 2)):
        for (k, _), copy in zip(plane, copies):
            if k == i:
                copy.wait_recv()
        ref = gath.at[moved(at, "x", 4 - i)["x"], :, c]
        across.append(remote(ref, ref, asend.at[15 + n], arecv.at[15 + n], sibling))
    loads[2].start()
    for copy in across:
        copy.wait_recv()

    squares = jnp.zeros((1, 128), F32)
    for i in range(4):
        for j in range(4):
            rows = gath[i, j].astype(F32).reshape(224, 128)
            squares = squares + jnp.sum(rows * rows, axis=0, keepdims=True)
    scale = lax.rsqrt(squares / D + norm_eps)
    gains = jnp.concatenate([pre_gain[...], jnp.zeros((100, 128), F32)], axis=0).T
    everything = gath[...].reshape(D, 128)
    for k in range(28):
        rows = everything[k * 128:(k + 1) * 128].astype(F32)
        norm_t[k * 128:(k + 1) * 128, :] = (rows * scale * gains[:, k:k + 1]).astype(BF16)

    loads[0].wait()
    loads[1].wait()
    gate = jnp.dot(wg[...], norm_t[...], preferred_element_type=F32)
    up = jnp.dot(wu[...], norm_t[...], preferred_element_type=F32)
    hidden[...] = (jax.nn.gelu(gate, approximate=True) * up).T.astype(BF16)

    loads[2].wait()
    copies = []
    for q in range(4):
        own = jnp.dot(hidden[...], wd[:, q * QUARTER:(q + 1) * QUARTER], preferred_element_type=F32)
        bp[:, :, q] = own.reshape(2, 4, 16, QUARTER)
        copies.append(remote(bp.at[1 - c, :, q], bp_in.at[:, q], bcsend.at[q], bcrecv.at[q], sibling))
    for q, copy in enumerate(copies):
        copy.wait_recv()
        bs[:, q] = (bp[c, :, q] + bp_in[:, q]).astype(BF16)
    copies = []
    for n, (i, j) in enumerate(plane):
        there = moved(moved(at, "x", i), "z", j)
        copies.append(
            remote(bs.at[there["x"], there["z"]], b_in.at[n], bsend.at[n], brecv.at[n], device(there))
        )
    loads[3].start()
    pick = lax.broadcasted_iota(jnp.int32, (16, 128), 0) + (c * 64 + x * 16)
    pick = (lax.broadcasted_iota(jnp.int32, (16, 128), 1) == pick).astype(BF16)
    mine = lax.dot_general(
        pick, own_rows(gath, z), (((1,), (1,)), ((), ())), preferred_element_type=F32
    )
    block = bp[c, x, z] + bp_in[x, z]
    for n, copy in enumerate(copies):
        copy.wait_recv()
        block = block + b_in[n].astype(F32)
    sums = jnp.broadcast_to(jnp.sum(block * block, axis=1, keepdims=True), (16, 128))
    sq[...] = sums
    copies = [
        remote(sq, sq_in.at[k - 1], sqsend.at[k - 1], sqrecv.at[k - 1], device(moved(at, "z", k)))
        for k in (1, 2, 3)
    ]
    for k, copy in enumerate(copies):
        copy.wait_recv()
        sums = sums + sq_in[k]
    row_scale = lax.rsqrt(sums[:, :1] / D + norm_eps)
    gain = lane_row(post_gain, z)
    block = mine + block * row_scale * gain
    for p in PIECES:
        layer[p][c, y, x, z] = block[:, OFFSETS[p]:OFFSETS[p] + WIDTHS[p]].astype(BF16)

    def gather(arrays, send, recv, lsend, lrecv, csend, crecv, use, known=0):
        stage, last, across = {}, {}, {}
        for step in range(known, 2):
            for p in WIDEST_FIRST:
                order = ORDERS[p]
                if step > known:
                    for copy in stage[p]:
                        copy.wait_recv()
                here = arrays[p].at[(c,) + grid_index(at, order[:step])]
                stage[p] = [
                    remote(here, here, send.at[step, p, k - 1], recv.at[step, p, k - 1],
                           device(moved(at, order[step], k)))
                    for k in (1, 2, 3)
                ]

        def pass_on(p, owner, half, steps, n):
            order = ORDERS[p]
            value = moved(at, order[2], owner)[order[2]]
            ref = arrays[p].at[(c,) + halves(at, order, value, half)]
            return remote(ref, ref, lsend.at[p, n], lrecv.at[p, n], device(moved(at, order[2], steps)))

        def cross(p, owner):
            ref = arrays[p].at[(c,) + grid_index(moved(at, ORDERS[p][2], owner), ORDERS[p][:2])]
            across[p].append(remote(ref, ref, csend.at[p, owner], crecv.at[p, owner], sibling))

        for p in WIDEST_FIRST:
            for copy in stage[p]:
                copy.wait_recv()
            last[p] = [
                pass_on(p, 0, 0, 1, 0), pass_on(p, 0, 1, 3, 1),
                pass_on(p, 0, 1, 1, 2), pass_on(p, 0, 0, 3, 3),
            ]
            across[p] = []
            cross(p, 0)
        for p in PIECES:
            last[p][0].wait_recv()
            last[p].append(pass_on(p, 3, 0, 1, 4))
            last[p][1].wait_recv()
            last[p].append(pass_on(p, 1, 1, 3, 5))
        for p in PIECES:
            last[p][2].wait_recv()
            cross(p, 3)
            last[p][3].wait_recv()
            cross(p, 1)

        def finish(p):
            last[p][4].wait_recv()
            last[p][5].wait_recv()
            cross(p, 2)

        finish(0)
        finish(1)
        use(0, c)
        finish(2)
        use(1, c)
        use(2, c)
        for p in PIECES:
            for copy in across[p]:
                copy.wait_recv()
            use(p, 1 - c)

    def encode(p, half):
        tokens = pl.ds(pl.multiple_of(half * 256, 256), 256)
        for q in range(4):
            low = q * QUARTER + OFFSETS[p]
            rows = layer[p][half, :, :, q].reshape(256, WIDTHS[p])
            more = jnp.dot(rows, we[low:low + WIDTHS[p], :], preferred_element_type=F32)
            if p == 0 and q == 0:
                pre[tokens, :] = b_enc[...] + more
            else:
                pre[tokens, :] += more

    loads[3].wait()
    loads[4].start()
    gather(layer, dsend, drecv, dlsend, dlrecv, dcsend, dcrecv, encode)

    pre_act = pre[...]
    soft = jax.nn.sigmoid((pre_act - threshold[...]) / gate_band)
    soft_s[...] = soft
    feat[...] = (pre_act * soft).astype(BF16)

    loads[4].wait()

    def partial(p):
        for q in range(4):
            low = q * QUARTER + OFFSETS[p]
            value = jnp.dot(feat[...], wdec[:, low:low + WIDTHS[p]], preferred_element_type=F32)
            part[p][:, :, :, q] = value.astype(BF16).reshape(2, 4, 4, 16, WIDTHS[p])
        copies[p] = remote(part[p].at[1 - c], part_in[p], pcsend.at[p], pcrecv.at[p], sibling)

    copies = {}
    stage = {}

    def reduce_first(p):
        copies[p].wait_recv()
        for i in range(4):
            total[p][i] = (part[p][c, i].astype(F32) + part_in[p][i].astype(F32)).astype(BF16)
        order = ORDERS[p]
        up, down = device(moved(at, order[2], 1)), device(moved(at, order[2], 3))
        value = {k: moved(at, order[2], k)[order[2]] for k in range(4)}

        def piece(k, half):
            return total[p].at[halves(at, order, value[k], half)]

        def first(src, dst, n, there):
            return remote(src, dst, fsend.at[p, n], frecv.at[p, n], there)

        stage[p] = [
            first(piece(2, 0), relay_in[p].at[0], 0, up),
            first(piece(2, 1), relay_in[p].at[1], 1, down),
            first(piece(1, 1), in_a[p].at[0, 2:4], 2, up),
            first(piece(3, 0), in_a[p].at[1, 0:2], 3, down),
        ]
    partial(2)
    partial(0)
    reduce_first(2)
    partial(1)
    reduce_first(0)
    reduce_first(1)
    soft = soft_s[...]
    gate_sum = jnp.broadcast_to(jnp.sum(soft).reshape(1, 1), (8, 128))
    gsum[0] = gate_sum
    gate_copies = [remote(gsum.at[0], gin.at[9], gsend.at[9], grecv.at[9], sibling)]
    for p in WIDEST_FIRST:
        order = ORDERS[p]
        up, down = moved(at, order[2], 1), moved(at, order[2], 3)
        for n, (there, half) in enumerate(((up, 0), (down, 1))):
            stage[p][n].wait_recv()
            own = total[p][halves(at, order, there[order[2]], half)].astype(F32)
            relay_out[p][n] = (own + relay_in[p][n].astype(F32)).astype(BF16)
            stage[p].append(
                remote(relay_out[p].at[n], in_a[p].at[n, 2 * half:2 * half + 2],
                       fsend.at[p, 4 + n], frecv.at[p, 4 + n], device(there))
            )

    gate_copies[0].wait_recv()
    gate_sum = gate_sum + gin[9]

    def gate_step(s, axis, value):
        gsum[1 + s] = value
        return [
            remote(gsum.at[1 + s], gin.at[3 * s + k - 1], gsend.at[3 * s + k - 1],
                   grecv.at[3 * s + k - 1], device(moved(at, axis, k)))
            for k in (1, 2, 3)
        ]

    def gate_finish(s, made, value):
        for k, copy in enumerate(made):
            copy.wait_recv()
            value = value + gin[3 * s + k]
        return value

    gate_copies = gate_step(0, "x", gate_sum)
    slope_s[...] = soft * (1.0 - soft) / gate_band
    feat_t[...] = feat[...].T
    outs = [pltpu.make_async_copy(feat_t, featt_out, osem.at[0])]
    outs[0].start()
    for p in PIECES:
        for q in range(4):
            low = q * QUARTER + OFFSETS[p]
            lt[low:low + WIDTHS[p], :] = layer[p][:, :, :, q].reshape(512, WIDTHS[p]).T
    outs.append(pltpu.make_async_copy(lt, lt_out, osem.at[1]))
    outs[1].start()
    for p in WIDEST_FIRST:
        last, second = ORDERS[p][2], ORDERS[p][1]
        for copy in stage[p][2:]:
            copy.wait_recv()
        value = total[p][grid_index(at, [a for a in "xyz" if a != last])].astype(F32)
        for k in range(2):
            value = value + in_a[p][k].astype(F32)
        sum_a[p][...] = value.astype(BF16)
        stage[p] = []
        left = [a for a in "yxz" if a != last]
        for k in (1, 2, 3):
            there = moved(at, second, k)
            src = sum_a[p].at[tuple(there[a] if a == second else slice(None) for a in left)]
            stage[p].append(
                remote(src, in_b[p].at[k - 1], rsend.at[0, p, k - 1], rrecv.at[0, p, k - 1], device(there))
            )
    gate_sum = gate_finish(0, gate_copies, gate_sum)
    gate_copies = gate_step(1, "y", gate_sum)
    for p in WIDEST_FIRST:
        last, second, first = ORDERS[p][2], ORDERS[p][1], ORDERS[p][0]
        for copy in stage[p]:
            copy.wait_recv()
        left = [a for a in "yxz" if a != last]
        value = sum_a[p][tuple(at[a] if a == second else slice(None) for a in left)].astype(F32)
        for k in range(3):
            value = value + in_b[p][k].astype(F32)
        value = value.astype(BF16)
        sum_b[p][...] = value
        in_c[p][at[first]] = value
        stage[p] = []
        for k in (1, 2, 3):
            stage[p].append(
                remote(sum_b[p], in_c[p].at[at[first]], rsend.at[1, p, k - 1],
                       rrecv.at[1, p, k - 1], device(moved(at, first, k)))
            )
    gate_sum = gate_finish(1, gate_copies, gate_sum)
    gate_copies = gate_step(2, "z", gate_sum)
    for p in PIECES:
        first = ORDERS[p][0]
        for copy in stage[p]:
            copy.wait_recv()
        for i in range(4):
            value = in_c[p][0, i].astype(F32)
            for k in (1, 2, 3):
                value = value + in_c[p][k, i].astype(F32)
            there = dict(at)
            there[first] = i
            bias = lane_row(b_dec, there["z"])
            value = value + bias[:, OFFSETS[p]:OFFSETS[p] + WIDTHS[p]]
            value = value - layer[p][c, there["y"], there["x"], there["z"]].astype(F32)
            err[p][c, there["y"], there["x"], there["z"]] = value.astype(BF16)

    def back(p, half):
        tokens = pl.ds(pl.multiple_of(half * 256, 256), 256)
        for q in range(4):
            low = q * QUARTER + OFFSETS[p]
            out = pltpu.make_async_copy(
                err[p].at[half, :, :, q], err_out.at[half, :, :, :, low:low + WIDTHS[p]],
                osem.at[len(outs)],
            )
            out.start()
            outs.append(out)
        for q in range(4):
            low = q * QUARTER + OFFSETS[p]
            more = lax.dot_general(
                err[p][half, :, :, q].reshape(256, WIDTHS[p]), wdec[:, low:low + WIDTHS[p]],
                (((1,), (1,)), ((), ())), preferred_element_type=F32,
            )
            if p == 0 and q == 0:
                gfeat[tokens, :] = more
            else:
                gfeat[tokens, :] += more

    gather(err, esend, erecv, elsend, elrecv, ecsend, ecrecv, back, 1)
    gate_out[...] = gate_finish(2, gate_copies, gate_sum)
    grad_feat = gfeat[...]
    side = (grad_feat * pre[...] + sparsity_coef) * slope_s[...]
    grad_pre = grad_feat * soft_s[...] + side
    thresh_out[...] = -jnp.sum(side, axis=0, keepdims=True)
    benc_out[...] = jnp.sum(grad_pre, axis=0, keepdims=True)
    gpre[...] = grad_pre.astype(BF16)
    outs.append(pltpu.make_async_copy(gpre, gpre_out, osem.at[26]))
    outs[-1].start()
    for copy in unsent:
        copy.wait_send()
    for out in outs:
        out.wait()


def own_rows(gath, z):
    return gath[pl.ds(z, 1)].reshape(QUARTER, 128)


def lane_row(ref, z):
    rows = [ref[pl.ds(z * 7 + i, 1), :] for i in range(7)]
    return jnp.concatenate(rows, axis=1)


def gradients(featt, gpre, gate_in, benc, thresh, err, lt, wdec_grad, wenc_grad, bdec_grad, loss,
              benc_grad, thresh_grad, square):
    step = pl.program_id(0)
    rows = err[...]
    wdec_grad[...] = jnp.dot(featt[...], rows, preferred_element_type=F32).astype(BF16)
    wenc_grad[...] = jnp.dot(lt[...], gpre[...], preferred_element_type=F32).astype(BF16)
    wide = rows.astype(F32)
    sums = jnp.sum(wide, axis=0, keepdims=True)
    for i in range(STEP // 128):
        bdec_grad[pl.ds(step * (STEP // 128) + i, 1), :] = sums[:, i * 128:(i + 1) * 128]
    more = jnp.sum(wide * wide, axis=0, keepdims=True)

    @pl.when(step == 0)
    def _():
        square[...] = more
        benc_grad[...] = benc[...]
        thresh_grad[...] = thresh[...]

    @pl.when(step > 0)
    def _():
        square[...] += more

    @pl.when(step == pl.num_programs(0) - 1)
    def _():
        loss[0] = (0.5 * jnp.sum(square[...]) + sparsity_coef * gate_in[0, 0]) / (512 * D)


def blocks(dtype=BF16, lead=(2, 4, 4, 4)):
    return [pltpu.VMEM(lead + (16, w), dtype) for w in WIDTHS]


STEP = 1792


def local(
    residual_in, pre_gain, post_gain, w_gate, w_up, w_down, w_enc, b_enc, threshold, w_dec, b_dec
):
    vmem = pl.BlockSpec(memory_space=pltpu.VMEM)
    hbm = pl.BlockSpec(memory_space=pl.ANY)
    dma = pltpu.SemaphoreType.DMA
    shape = jax.ShapeDtypeStruct
    square = lambda dtype: pltpu.VMEM((512, 512), dtype)
    err, lt, featt, gpre, gate_total, benc, thresh = pl.pallas_call(
        forward,
        out_shape=[
            shape((2, 4, 4, 16, D), BF16), shape((D, 512), BF16), shape((512, 512), BF16),
            shape((512, 512), BF16), shape((8, 128), F32), shape((1, 512), F32), shape((1, 512), F32),
        ],
        in_specs=[hbm] * 11,
        out_specs=[hbm] * 4 + [vmem] * 3,
        scratch_shapes=[
            *[pltpu.VMEM((28, 128), F32)] * 3, *[pltpu.VMEM((1, 512), F32)] * 2,
            pltpu.VMEM((448, D), BF16), pltpu.VMEM((448, D), BF16), pltpu.VMEM((448, D), BF16),
            pltpu.VMEM((D, 512), BF16), pltpu.VMEM((512, D), BF16),
            pltpu.VMEM((4, 4, 2, 112, 128), BF16), pltpu.VMEM((D, 128), BF16),
            pltpu.VMEM((128, 448), BF16),
            pltpu.VMEM((2, 4, 4, 16, QUARTER), F32), pltpu.VMEM((4, 4, 16, QUARTER), F32),
            pltpu.VMEM((4, 4, 16, QUARTER), BF16), pltpu.VMEM((15, 16, QUARTER), BF16),
            pltpu.VMEM((16, 128), F32), pltpu.VMEM((3, 16, 128), F32),
            *blocks(), square(BF16), square(BF16), square(F32), square(F32), square(F32), square(F32),
            square(BF16), pltpu.VMEM((D, 512), BF16),
            *blocks(), *blocks(lead=(4, 4, 4)), *blocks(lead=(4, 4, 4)),
            *blocks(lead=(2, 4, 4)), *blocks(lead=(2, 2, 4)), *blocks(lead=(2, 2, 4)),
            *blocks(lead=(4, 4)), *blocks(lead=(3, 4)), *blocks(lead=(4,)), *blocks(lead=(4, 4)),
            *blocks(), pltpu.VMEM((4, 8, 128), F32), pltpu.VMEM((10, 8, 128), F32),
            dma((11,)), dma((19,)), dma((19,)), dma((4,)), dma((4,)), dma((15,)), dma((15,)),
            dma((3,)), dma((3,)),
            dma((2, 3, 3)), dma((2, 3, 3)), dma((3, 6)), dma((3, 6)), dma((3, 4)), dma((3, 4)),
            dma((3,)), dma((3,)), dma((3, 6)), dma((3, 6)), dma((2, 3, 3)), dma((2, 3, 3)),
            dma((2, 3, 3)), dma((2, 3, 3)), dma((3, 6)), dma((3, 6)), dma((3, 4)), dma((3, 4)),
            dma((10,)), dma((10,)), dma((27,)),
        ],
        compiler_params=pltpu.CompilerParams(
            collective_id=0, has_side_effects=True, vmem_limit_bytes=58 * 1024 * 1024
        ),
        name="forward",
    )(
        residual_in.T, pre_gain.reshape(28, 128), post_gain.reshape(28, 128), b_dec.reshape(28, 128),
        b_enc.reshape(1, 512), threshold.reshape(1, 512), w_gate.T, w_up.T, w_down, w_enc, w_dec,
    )
    fixed = lambda dims: pl.BlockSpec(dims, lambda i: (0, 0))
    across = pl.BlockSpec((512, STEP), lambda i: (0, i))
    along = pl.BlockSpec((STEP, 512), lambda i: (i, 0))
    grads = pl.pallas_call(
        gradients,
        grid=(D // STEP,),
        out_shape=[
            shape((512, D), BF16), shape((D, 512), BF16), shape((28, 128), F32), shape((1,), F32),
            shape((1, 512), F32), shape((1, 512), F32),
        ],
        in_specs=[
            fixed((512, 512)), fixed((512, 512)), fixed((8, 128)), fixed((1, 512)), fixed((1, 512)),
            across, along,
        ],
        out_specs=[
            across, along, fixed((28, 128)),
            pl.BlockSpec(memory_space=pltpu.SMEM), fixed((1, 512)), fixed((1, 512)),
        ],
        scratch_shapes=[pltpu.VMEM((1, STEP), F32)],
        compiler_params=pltpu.CompilerParams(vmem_limit_bytes=60 * 1024 * 1024),
        name="gradients",
    )(featt, gpre, gate_total, benc, thresh, err.reshape(512, D), lt)
    return (
        grads[3].reshape(()), grads[1], grads[0], grads[4].reshape(512), grads[5].reshape(512),
        grads[2].reshape(D),
    )


def solution(mesh):
    placed = (
        P("dp", "mp"),
        P(),
        P(),
        P(None, "mp"),
        P(None, "mp"),
        P("mp", None),
        P(None, ("dp", "mp")),
        P(("dp", "mp")),
        P(("dp", "mp")),
        P(("dp", "mp"), None),
        P(),
    )
    return jax.shard_map(
        local,
        mesh=mesh,
        in_specs=placed,
        out_specs=(
            P(),
            P(None, ("dp", "mp")),
            P(("dp", "mp"), None),
            P(("dp", "mp")),
            P(("dp", "mp")),
            P(),
        ),
        check_vma=False,
    )
```
